512 devices in a mesh: seq: 32 (over z, x), dp: 2 (over core), tensor: 8 (over y).
Axes of the slice: x: 4, y: 8, z: 8, core: 2. Of those that a mesh axis runs over, the one named last changes fastest.
Arguments:
- head_inputs: bfloat16 [2, 2560, 16384], P('dp', 'tensor', 'seq'), may hold values from -6 to 6
- b_proj: bfloat16 [2, 16384, 128], P('dp', 'seq'), may hold values from -0.59765625 to 0.59765625
- c_proj: bfloat16 [2, 16384, 128], P('dp', 'seq'), may hold values from -0.59765625 to 0.59765625
- dt_raw: float32 [2, 40, 16384], P('dp', 'tensor', 'seq'), may hold values from -2 to 0
- a_log: float32 [40], P('tensor'), as said below
- d_skip: float32 [40], P('tensor'), may hold values from 0.5 to 1.5
- w_out: bfloat16 [2560, 2560], P('tensor', 'dp'), may hold values from -0.125 to 0.125
- out_grad: bfloat16 [2, 2560, 16384], P('dp', 'tensor', 'seq'), may hold values from -6 to 6
Outputs:
- mixed: bfloat16 [2, 2560, 16384], P('dp', 'tensor', 'seq')
- grad_inputs: bfloat16 [2, 2560, 16384], P('dp', 'tensor', 'seq')
- grad_b: bfloat16 [2, 16384, 128], P('dp', 'seq')
- grad_c: bfloat16 [2, 16384, 128], P('dp', 'seq')
- grad_dt: float32 [2, 40, 16384], P('dp', 'tensor', 'seq')
- grad_alog: float32 [40], P('tensor')
- grad_skip: float32 [40], P('tensor')
- grad_w: bfloat16 [2560, 2560], P('tensor', ('seq', 'dp'))
The draws below stay inside these ranges and needn't reach their ends.
Inputs may be any that keep to these rules, and one draw needn't show every extreme that they name: exp(a_log) lies between 0.1 / 16384 and 0.1.
All inputs are finite; a program needn't handle non-finite values.
Results may differ from the reference program's by a relative error of at most 0.0049.
Values may be sent and summed in bfloat16 or wider, within the bound.
A program may use at most 128 MiB of HBM per device.

```python
import math
import jax
import jax.numpy as jnp
from jax import lax

HEADS = 40
HEAD_DIM = 64
STATE = 128
SPAN = 256
D_OUT = 2560
SEQ_LEN = 16384
ROLLOUTS = 2
HP = 2560
N_DP = 2
N_TENSOR = 8


def draw_a_log(key, part):
    spots = jax.random.uniform(key, (HEADS,), jnp.float32)
    lower = math.log(0.1 / SEQ_LEN)
    upper = math.log(0.1)
    return lower + (upper - lower) * spots


def raised(result, rng, source, target, parts, factor):
    def block_of(axis_at):
        return (jnp.arange(result.shape[axis_at]) // (result.shape[axis_at] // parts)).reshape((-1,) + (1,) * (result.ndim - 1 - axis_at))

    one_side = jax.random.permutation(rng, parts)[block_of(target)]
    second = (block_of(target) + parts // 2) % parts
    return jnp.where((block_of(source) == one_side) | (block_of(source) == second), factor * result, result)


def shard_levels(own_key, extent, pieces, low, high):
    def one(axis_at, blocks):
        draws = jax.random.uniform(jax.random.fold_in(jax.random.fold_in(own_key, 6), axis_at), (blocks,), jnp.float32, low / len(pieces), high / len(pieces))
        return jnp.repeat(jnp.exp(draws), extent[axis_at] // blocks).reshape((-1,) + (1,) * (len(extent) - axis_at - 1))

    loudness = one(*pieces[0])
    for cut in pieces[1:]:
        loudness = loudness * one(*cut)
    return loudness


def scatter_about(rng, dims, deviation, most, shards=(), kind=jnp.bfloat16):
    gain = shard_levels(rng, dims, shards, -0.22, 0.18) if shards else 1.0
    values = jax.random.normal(rng, dims, jnp.float32) * deviation * gain
    return jnp.minimum(jnp.maximum(values, -most), most).astype(kind)


def noise_with(rng, extent, deviation, reach, pieces, heavy, held_as=jnp.bfloat16):
    values = deviation * jax.random.normal(rng, extent, jnp.float32)
    if pieces:
        values = values * shard_levels(rng, extent, pieces, -0.22, 0.18)
    return jnp.clip(raised(values, jax.random.fold_in(rng, 3), *heavy), -reach, reach).astype(held_as)


def setup_inputs(seed: int = 0) -> dict:
    keys = jax.random.split(jax.random.key(seed), 9)
    return {
        "head_inputs": scatter_about(keys[0], (ROLLOUTS, HP, SEQ_LEN), 1.0, 6.0, ((0, 2), (1, 8), (2, 32))),
        "b_proj": scatter_about(keys[1], (ROLLOUTS, SEQ_LEN, STATE), 0.1, 0.59765625, ((0, 2), (1, 32))),
        "c_proj": scatter_about(keys[2], (ROLLOUTS, SEQ_LEN, STATE), 0.1, 0.59765625, ((0, 2), (1, 32))),
        "dt_raw": jnp.clip(-2.0 + 2.0 * jax.random.uniform(keys[3], (ROLLOUTS, HEADS, SEQ_LEN), jnp.float32) ** shard_levels(keys[3], (ROLLOUTS, HEADS, SEQ_LEN), ((0, 2), (1, 8), (2, 32)), -0.2, 0.2), -2.0, 0.0),
        "a_log": draw_a_log(jax.random.fold_in(keys[8], 71), 0),
        "d_skip": jnp.clip(0.5 + 1.0 * jax.random.uniform(keys[5], (HEADS,), jnp.float32) ** shard_levels(keys[5], (HEADS,), ((0, 8),), -0.2, 0.2), 0.5, 1.5),
        "w_out": scatter_about(keys[6], (HP, D_OUT), D_OUT ** -0.5, 0.125, ((0, 8), (1, 2))),
        "out_grad": noise_with(keys[7], (ROLLOUTS, D_OUT, SEQ_LEN), 1.0, 6.0, ((0, 2), (1, 8), (2, 32)), (2, 1, 32, 2.75)),
    }


HIGH = lax.Precision.HIGHEST

def span_pass(carried, x_block, b_block, c_block, step_block, decay_rate):
    log_decay = step_block * decay_rate[:, None]
    cumulative = jnp.cumsum(log_decay, axis=1)
    block = cumulative.shape[1]
    indices = jnp.arange(block)
    causal = (indices[:, None] >= indices[None, :])[None, :, :]
    spread = cumulative[:, :, None] - cumulative[:, None, :]
    weights = jnp.where(causal, jnp.exp(jnp.where(causal, spread, 0.0)), 0.0)
    affinity = jnp.dot(c_block, b_block.T, precision=HIGH)
    scores = affinity[None, :, :] * weights * step_block[:, None, :]
    block_out = jnp.einsum('hps,hts->hpt', x_block, scores, precision=HIGH)
    block_out = block_out + jnp.exp(cumulative)[:, None, :] * jnp.einsum('hpn,tn->hpt', carried, c_block, precision=HIGH)
    tail_weight = jnp.exp(cumulative[:, -1:] - cumulative) * step_block
    updated = jnp.exp(cumulative[:, -1])[:, None, None] * carried
    updated = updated + jnp.einsum('hps,sn->hpn', x_block * tail_weight[:, None, :], b_block, precision=HIGH)
    return (updated, block_out)

def sweep(streams, b_rows, c_rows, dt_rows, alog_part, skip_part, state_in):
    head_count, head_width, length = streams.shape
    blocks = length // SPAN
    step_size = jax.nn.softplus(dt_rows)
    decay_rate = -jnp.exp(alog_part)
    x_blocks = streams.reshape(head_count, head_width, blocks, SPAN).transpose(2, 0, 1, 3)
    b_blocks = b_rows.reshape(blocks, SPAN, b_rows.shape[1])
    c_blocks = c_rows.reshape(blocks, SPAN, c_rows.shape[1])
    s_blocks = step_size.reshape(head_count, blocks, SPAN).transpose(1, 0, 2)

    def advance(carried, inputs):
        return span_pass(carried, inputs[0], inputs[1], inputs[2], inputs[3], decay_rate)
    state_end, outputs = lax.scan(advance, state_in, (x_blocks, b_blocks, c_blocks, s_blocks))
    mixed_f = outputs.transpose(1, 2, 0, 3).reshape(head_count, head_width, length)
    return (mixed_f + skip_part[:, None, None] * streams, state_end)

def reference(head_inputs, b_proj, c_proj, dt_raw, a_log, d_skip, w_out, out_grad):
    group_size = HEADS // N_TENSOR
    mixed_all = []
    gin_all = []
    gb_all = []
    gc_all = []
    gdt_all = []
    alog_total = jnp.zeros((HEADS,), jnp.float32)
    skip_total = jnp.zeros((HEADS,), jnp.float32)
    w_total = jnp.zeros((HP, D_OUT), jnp.float32)
    for rollout in range(N_DP):
        cotan_half = jnp.dot(w_out, out_grad[rollout], preferred_element_type=jnp.float32).astype(jnp.bfloat16)
        y_cotan = lax.optimization_barrier(cotan_half).astype(jnp.float32)
        b_rows = b_proj[rollout].astype(jnp.float32)
        c_rows = c_proj[rollout].astype(jnp.float32)
        streams = head_inputs[rollout].astype(jnp.float32).reshape(N_TENSOR, group_size, HEAD_DIM, SEQ_LEN)
        cotans = y_cotan.reshape(N_TENSOR, group_size, HEAD_DIM, SEQ_LEN)
        dt_groups = dt_raw[rollout].reshape(N_TENSOR, group_size, SEQ_LEN)
        alog_groups = a_log.reshape(N_TENSOR, group_size)
        skip_groups = d_skip.reshape(N_TENSOR, group_size)

        def per_group(running, inputs):
            start_state = jnp.zeros((group_size, HEAD_DIM, STATE), jnp.float32)

            def forward(xa, ba, ca, da, aa, sa):
                return sweep(xa, ba, ca, da, aa, sa, start_state)[0]
            primal, pullback = jax.vjp(forward, inputs[0], b_rows, c_rows, inputs[2], inputs[3], inputs[4])
            grads = pullback(inputs[1])
            return ((running[0] + grads[1], running[1] + grads[2]), (primal, grads[0], grads[3], grads[4], grads[5]))
        zero_rows = jnp.zeros((SEQ_LEN, STATE), jnp.float32)
        sums, results = lax.scan(per_group, (zero_rows, zero_rows), (streams, cotans, dt_groups, alog_groups, skip_groups))
        mixed_half = results[0].reshape(HP, SEQ_LEN).astype(jnp.bfloat16)
        mixed_all.append(mixed_half)
        gin_all.append(results[1].reshape(HP, SEQ_LEN).astype(jnp.bfloat16))
        gb_all.append(sums[0].astype(jnp.bfloat16))
        gc_all.append(sums[1].astype(jnp.bfloat16))
        gdt_all.append(results[2].reshape(HEADS, SEQ_LEN))
        alog_total = alog_total + results[3].reshape(HEADS)
        skip_total = skip_total + results[4].reshape(HEADS)
        w_total = w_total + lax.dot_general(mixed_half, out_grad[rollout], (((1,), (1,)), ((), ())), preferred_element_type=jnp.float32)
    return (jnp.stack(mixed_all), jnp.stack(gin_all), jnp.stack(gb_all), jnp.stack(gc_all), jnp.stack(gdt_all), alog_total, skip_total, w_total.astype(jnp.bfloat16))
```

```python
import functools
import types

import jax
import jax.numpy as jnp
from jax import lax
from jax.experimental import pallas as pl
from jax.experimental.pallas import tpu as pltpu
from jax.sharding import PartitionSpec as P

F32 = jnp.float32
BF16 = jnp.bfloat16
CHUNKS = 4
NN = (((1,), (0,)), ((), ()))
NT = (((1,), (1,)), ((), ()))
TN = (((0,), (0,)), ((), ()))


def mul(a, b, dims):
    return lax.dot_general(a, b, dims, preferred_element_type=F32)


def split(v):
    hi = v.astype(BF16)
    return hi, (v - hi.astype(F32)).astype(BF16)


def mul3(a, b, dims):
    return mul(a[0], b[0], dims) + mul(a[1], b[0], dims) + mul(a[0], b[1], dims)


def mul2(a, b, dims):
    return mul(a[0], b, dims) + mul(a[1], b, dims)


def prefix_sum(v, reverse=False):
    length = v.shape[1]
    lane = lax.broadcasted_iota(jnp.int32, v.shape, 1)
    shift = 1
    while shift < length:
        if reverse:
            moved = pltpu.roll(v, length - shift, 1)
            v = v + jnp.where(lane < length - shift, moved, 0.0)
        else:
            moved = pltpu.roll(v, shift, 1)
            v = v + jnp.where(lane >= shift, moved, 0.0)
        shift *= 2
    return v


def space(d):
    return types.SimpleNamespace(**{k: space(v) if isinstance(v, dict) else v for k, v in d.items()})


def kernel(dims, names, tree, *refs):
    nz, nx, ny, heads, width, length, state = dims
    r = space(
        dict(zip(names, refs[: len(names)], strict=True))
        | jax.tree.unflatten(tree, refs[len(names) :])
    )
    x_ref, b_ref, c_ref = r.x_in, r.b_in, r.c_in
    rows_all = heads * width
    rp = width // nx
    fx = rows_all // nx
    seq = lax.axis_index("seq")
    core = lax.axis_index("dp")
    y = lax.axis_index("tensor")
    z = lax.div(seq, nx)
    x = lax.rem(seq, nx)
    sends, stores = [], []

    def wrap(i, n):
        return lax.rem(i + n, n)

    def copy(src, dst, ch, out, into, where):
        return pltpu.make_async_remote_copy(
            src_ref=src,
            dst_ref=dst,
            send_sem=ch.s.at[out],
            recv_sem=ch.r.at[into],
            device_id=where,
            device_id_type=pl.DeviceIdType.MESH,
        )

    def start(*a):
        c = copy(*a)
        c.start()
        sends.append(c)

    def at_x(i):
        return {"seq": z * nx + i}

    def at_z(i):
        return {"seq": i * nx + x}

    def at_y(i):
        return {"tensor": i}

    other = {"dp": 1 - core}

    def exchange(n, me, place, src, dst, ch):
        for k in range(1, n):
            p = wrap(me + k, n)
            start(src(p), dst(me), ch, (p,), (me,), place(p))

    def arrived(n, me, place, src, dst, ch):
        for k in range(1, n):
            p = wrap(me + k, n)
            copy(src(p), dst(p), ch, (p,), (p,), place(p)).wait_recv()

    def store(src, dst):
        c = pltpu.make_async_copy(src, dst, r.stores.at[len(stores)])
        c.start()
        stores.append(c)

    def head(h):
        return slice(h * width, (h + 1) * width)

    g_all = r.g_all
    own_rows = g_all.at[pl.ds(pl.multiple_of(y * rows_all, 16), rows_all), :]
    loads = [
        pltpu.make_async_copy(src, dst, r.load.at[i])
        for i, (src, dst) in enumerate(
            ((r.dt, r.dt_in), (r.x, x_ref), (r.b, b_ref), (r.c, c_ref), (r.w, r.w_in), (r.g, own_rows))
        )
    ]
    for c in loads:
        c.start()

    barrier = pltpu.get_barrier_semaphore()
    peers = [at_x(wrap(x + k, nx)) for k in range(1, nx)]
    peers += [at_z(wrap(z + k, nz)) for k in range(1, nz)]
    peers += [at_y(wrap(y + k, ny)) for k in range(1, ny)] + [other]
    for p in peers:
        pl.semaphore_signal(barrier, inc=1, device_id=p, device_id_type=pl.DeviceIdType.MESH)
    pl.semaphore_wait(barrier, len(peers))

    far = ny // 2
    tall = rows_all // CHUNKS

    def block(t, c):
        return g_all.at[pl.ds(pl.multiple_of(t * rows_all + c * tall, 16), tall), :]

    def forward(k, c, way):
        if k + 1 > far or (k + 1 == far and (c < CHUNKS // 2) != (way == 0)):
            return
        t = wrap(y - k, ny) if way == 0 else wrap(y + k, ny)
        to = wrap(y + 1, ny) if way == 0 else wrap(y - 1, ny)
        src = r.g.at[pl.ds(c * tall, tall), :] if k == 0 else block(t, c)
        start(src, block(t, c), r.ch.g, (way, k, c,), (t, c,), at_y(to))

    def block_in(t, c):
        copy(block(t, c), block(t, c), r.ch.g, (0, 0, 0,), (t, c,), at_y(y)).wait_recv()

    def relay(k, chunks):
        for c in chunks:
            if k == far:
                block_in(wrap(y + k, ny), c)
                continue
            block_in(wrap(y - k, ny), c)
            forward(k, c, 0)
            block_in(wrap(y + k, ny), c)
            forward(k, c, 1)

    for c in range(CHUNKS):
        forward(0, c, 0)
        forward(0, c, 1)
    start(r.w, r.w_other, r.ch.w, (0,), (0,), other)

    tile = r.dt_rows
    tile[...] = jnp.zeros_like(tile)
    loads[0].wait()
    for h in range(heads):
        tile[h : h + 1, :] = r.dt_in[h]
    rate_rows = r.rate_rows
    rate_rows[...] = jnp.zeros_like(rate_rows)
    for h in range(heads):
        rate_rows[h : h + 1, :] = -jnp.exp(jnp.full((1, length), r.alog[h], F32))
    dt = tile[...]
    rate = rate_rows[...]
    grown = jnp.exp(dt)
    step = jnp.log(1.0 + grown)
    log_decay = step * rate
    cum = prefix_sum(log_decay)
    up = jnp.exp(cum)
    into = step * jnp.exp(-cum)
    decay_x, decay_z = r.decay_x, r.decay_z
    decay_x[x] = jnp.broadcast_to(up[:, length - 1 : length], (8, 128))
    exchange(nx, x, at_x, lambda p: decay_x.at[x], lambda p: decay_x.at[p], r.ch.dx)

    xs_h, xs_l = r.xs_h, r.xs_l
    loads[1].wait()
    for h in range(heads):
        hi, lo = split(x_ref[head(h), :].astype(F32) * into[h : h + 1, :])
        xs_h[head(h), :] = hi
        xs_l[head(h), :] = lo

    loads[2].wait()
    part = mul2((xs_h[...], xs_l[...]), b_ref[...], NN)
    mine = decay_x[x]
    ends = r.ends
    for h in range(heads):
        ends[h] = part[head(h), :] * mine[h : h + 1, :]

    def piece(ref, i):
        return ref.at[:, pl.ds(pl.multiple_of(i * rp, rp), rp), :]

    def cut(ref, i):
        return ref[:, pl.ds(pl.multiple_of(i * rp, rp), rp), :]

    def along_x(src, st):
        got = st.got1
        exchange(nx, x, at_x, lambda p: piece(src, p), lambda p: got.at[p], st.ch1)
        got[x] = cut(src, x)

    def along_z(src, st, back):
        got, tot = st.got1, st.tot
        arrived(nx, x, at_x, lambda p: piece(src, p), lambda p: got.at[p], st.ch1)
        for h in range(heads):
            acc = jnp.zeros((rp, state), F32)
            for j in reversed(range(nx)) if back else range(nx):
                acc = acc * decay_x[j, h : h + 1, :] + got[j, h].astype(F32)
            tot[h] = acc.astype(tot.dtype)
        for k in range(1, nz):
            p = z - k if back else z + k

            @pl.when(p >= 0 if back else p < nz)
            def _(p=p):
                copy(tot, st.got2.at[z], st.ch2, (p,), (z,), at_z(p)).start()

    def back_along_x(dst, st, back):
        got, tot, acc, out = st.got1, st.tot, st.acc, st.got3
        acc[...] = jnp.zeros_like(acc)

        def gather(i, carry):
            p = nz - 1 - i if back else i
            slot = st.got2.at[p]
            copy(tot, slot, st.ch2, (p,), (p,), at_z(p)).wait_recv()
            for h in range(heads):
                acc[h] = acc[h] * decay_z[p, h : h + 1, :] + st.got2[p, h].astype(F32)
            return carry

        lax.fori_loop(0, nz - 1 - z if back else z, gather, 0)
        for h in range(heads):
            s = acc[h]
            for j in reversed(range(nx)) if back else range(nx):
                out[j, h] = s.astype(out.dtype)
                s = s * decay_x[j, h : h + 1, :] + got[j, h].astype(F32)
        for k in range(1, nx):
            p = wrap(x + k, nx)
            start(out.at[p], piece(dst, x), st.ch3, (p,), (x,), at_x(p))
        dst[:, pl.ds(pl.multiple_of(x * rp, rp), rp), :] = out[x]

    def in_from_x(dst, st):
        for k in range(1, nx):
            p = wrap(x + k, nx)
            copy(st.got3.at[p], piece(dst, p), st.ch3, (p,), (p,), at_x(p)).wait_recv()

    def z_sent(st, back):
        for k in range(1, nz):
            p = z - k if back else z + k

            @pl.when(p >= 0 if back else p < nz)
            def _(p=p):
                copy(st.tot, st.got2.at[z], st.ch2, (p,), (z,), at_z(p)).wait_send()

    along_x(ends, r.ahead)
    arrived(nx, x, at_x, lambda p: decay_x.at[x], lambda p: decay_x.at[p], r.ch.dx)
    group = decay_x[0]
    for j in range(1, nx):
        group = group * decay_x[j]
    decay_z[z] = group
    exchange(nz, z, at_z, lambda p: decay_z.at[z], lambda p: decay_z.at[p], r.ch.dz)

    loads[3].wait()
    earlier = lax.broadcasted_iota(jnp.int32, (length, length), 0) >= lax.broadcasted_iota(
        jnp.int32, (length, length), 1
    )
    near_h, near_l = r.near_h, r.near_l
    hi, lo = split(jnp.where(earlier, mul(c_ref[...], b_ref[...], NT), 0.0))
    near_h[...] = hi
    near_l[...] = lo

    w_block, cotan_f = r.w_block, r.cotan_f
    per_core = ny // 2

    def w_blocks(ref, d):
        for i in range(per_core):
            w_block[d * per_core + i] = ref[:, i * rows_all : (i + 1) * rows_all]

    def term(k):
        t = wrap(y + k, ny)
        return mul(w_block[t], g_all[pl.ds(pl.multiple_of(t * rows_all, 16), rows_all), :], NN)

    early, late = range(CHUNKS // 2), range(CHUNKS // 2, CHUNKS)
    if far > 1:
        relay(1, early)
    along_z(ends, r.ahead, False)
    if far > 1:
        relay(1, late)
    loads[4].wait()
    w_blocks(r.w_in, core)
    copy(r.w, r.w_other, r.ch.w, (0,), (0,), other).wait_recv()
    w_blocks(r.w_other, 1 - core)
    loads[5].wait()
    cotan_f[...] = term(0)
    if far > 1:
        cotan_f[...] += term(1) + term(-1)
    arrived(nz, z, at_z, lambda p: decay_z.at[z], lambda p: decay_z.at[p], r.ch.dz)
    start_state = r.start_state
    if far > 2:
        relay(2, range(CHUNKS))
        cotan_f[...] += term(2) + term(-2)
    back_along_x(start_state, r.ahead, False)
    if far > 3:
        relay(3, range(CHUNKS))
        cotan_f[...] += term(3) + term(-3)
    in_from_x(start_state, r.ahead)

    s_h, s_l = split(start_state[...].reshape(rows_all, state))
    r.s_h[...] = s_h
    r.s_l[...] = s_l
    summed = mul3((xs_h[...], xs_l[...]), (near_h[...], near_l[...]), NT) + mul2((s_h, s_l), c_ref[...], NT)
    mixed = r.mixed
    past = r.past
    for h in range(heads):
        v = summed[head(h), :] * up[h : h + 1, :]
        past[head(h), :] = v
        mixed[head(h), :] = (v + r.skip[h] * x_ref[head(h), :].astype(F32)).astype(BF16)

    store(mixed, r.to_mixed)

    evens = [0] + [s * k for k in range(2, far, 2) for s in (1, -1)] + ([far] if far % 2 == 0 else [])
    odds = [s * k for k in range(1, far, 2) for s in (1, -1)] + ([far] if far % 2 == 1 else [])
    same = lax.rem(y + core, 2) == 0
    gw_dp, gw_out, gw_send, gw_x, gw_z = r.gw_dp, r.gw_out, r.gw_send, r.gw_x, r.gw_z

    def product(t):
        return mul(g_all[pl.ds(pl.multiple_of(t * rows_all, 16), rows_all), :], mixed[...], NT)

    def kept(j):
        return wrap(jnp.where(same, y + evens[j], y + odds[j]), ny)

    def w_pair(j):
        t = wrap(jnp.where(same, y + odds[j], y + evens[j]), ny)
        gw_out[j] = product(t).astype(BF16)
        start(gw_out.at[j], gw_dp.at[j], r.ch.wd, (j,), (j,), other)
        r.gw_own[j] = product(kept(j))

    def w_rows(j, p):
        return gw_send.at[j, pl.ds(pl.multiple_of(p * fx, 16), fx), :]

    def w_along_x(j):
        copy(gw_out.at[j], gw_dp.at[j], r.ch.wd, (j,), (j,), other).wait_recv()
        gw_send[j] = (r.gw_own[j] + gw_dp[j].astype(F32)).astype(BF16)
        for k in range(1, nx):
            p = wrap(x + k, nx)
            start(w_rows(j, p), gw_x.at[j, x], r.ch.wx, (j, p,), (j, x,), at_x(p))

    def w_along_z(j):
        total = gw_send[j, pl.ds(pl.multiple_of(x * fx, 16), fx), :].astype(F32)
        for k in range(1, nx):
            p = wrap(x + k, nx)
            copy(w_rows(j, p), gw_x.at[j, p], r.ch.wx, (j, p,), (j, p,), at_x(p)).wait_recv()
            total = total + gw_x[j, p].astype(F32)
        t = kept(j)
        gw_z_out = r.gw_z_out
        gw_z_out[j] = total.astype(BF16)

        @pl.when(t == z)
        def _():
            gw_z[z] = gw_z_out[j]

        @pl.when(t != z)
        def _():
            copy(gw_z_out.at[j], gw_z.at[z], r.ch.wz, (j,), (z,), at_z(t)).start()

    pairs = len(evens)
    for j in range(pairs - 1):
        w_pair(j)
    relay(far, range(CHUNKS))

    cotan = r.cotan
    cotan[...] = (cotan_f[...] + term(far)).astype(BF16)
    cs_h, cs_l = r.cs_h, r.cs_l
    for h in range(heads):
        hi, lo = split(cotan[head(h), :].astype(F32) * up[h : h + 1, :])
        cs_h[head(h), :] = hi
        cs_l[head(h), :] = lo
    starts = r.starts
    starts[...] = mul2((cs_h[...], cs_l[...]), c_ref[...], NN).reshape(heads, width, state).astype(starts.dtype)
    along_x(starts, r.behind)

    for j in range(pairs - 1):
        w_along_x(j)
    w_pair(pairs - 1)

    hi, lo = split(jnp.where(earlier, mul3((cs_h[...], cs_l[...]), (xs_h[...], xs_l[...]), TN), 0.0))
    near_gh, near_gl = r.near_gh, r.near_gl
    near_gh[...] = hi
    near_gl[...] = lo
    along_z(starts, r.behind, True)

    piece_rows = length // ny

    def tokens(ref, p):
        return ref.at[pl.ds(pl.multiple_of(p * piece_rows, 16), piece_rows), :]

    grad_c = mul2((near_gh[...], near_gl[...]), b_ref[...], NN) + mul3(
        (cs_h[...], cs_l[...]), (r.s_h[...], r.s_l[...]), TN
    )

    def over_y(v, st):
        send = st.out
        send[...] = v.astype(BF16)
        exchange(ny, y, at_y, lambda p: tokens(send, p), lambda p: st.got.at[p], st.ch)

    def back_over_y(st):
        send, got, full = st.out, st.got, st.full
        arrived(ny, y, at_y, lambda p: tokens(send, p), lambda p: got.at[p], st.ch)
        total = send[pl.ds(pl.multiple_of(y * piece_rows, 16), piece_rows), :].astype(F32)
        for k in range(1, ny):
            total = total + got[wrap(y + k, ny)].astype(F32)
        full[pl.ds(pl.multiple_of(y * piece_rows, 16), piece_rows), :] = total.astype(BF16)
        exchange(ny, y, at_y, lambda p: tokens(full, y), lambda p: tokens(full, p), st.chf)

    def in_over_y(st, out):
        full = st.full
        arrived(ny, y, at_y, lambda p: tokens(full, y), lambda p: tokens(full, p), st.chf)
        store(full, out)

    over_y(grad_c, r.sgc)
    w_along_x(pairs - 1)

    xg = r.xg
    xg[...] = mul3((cs_h[...], cs_l[...]), (near_h[...], near_l[...]), NN)
    grad_b = r.grad_b
    grad_b[...] = mul2((near_gh[...], near_gl[...]), c_ref[...], TN)
    to_in, to_cum, end_part, head_part = r.to_in, r.to_cum, r.end_part, r.head_part
    for ref in (to_in, to_cum, end_part, head_part):
        ref[...] = jnp.zeros_like(ref)
    total = cum[:, length - 1 : length]
    left_h, left_l = r.left_h, r.left_l
    for h in range(heads):
        xf = x_ref[head(h), :].astype(F32)
        gf = cotan[head(h), :].astype(F32)
        xs = xf * into[h : h + 1, :]
        inner = jnp.sum(xg[head(h), :] * xs, axis=0, keepdims=True)
        here = jnp.sum(gf * r.past[head(h), :], axis=0, keepdims=True) - inner
        to_cum[h : h + 1, :] = here
        skip_sum = jnp.sum(jnp.sum(gf * xf, axis=0, keepdims=True), axis=1, keepdims=True)
        decay_sum = jnp.sum(here * cum[h : h + 1, :], axis=1, keepdims=True)
        spot = lax.broadcasted_iota(jnp.int32, (1, 128), 1) == h
        head_part[0:1, :] += jnp.where(spot, decay_sum, 0.0)
        head_part[1:2, :] += jnp.where(spot, skip_sum, 0.0)
        hi, lo = split(xs * (total[h : h + 1, :] - cum[h : h + 1, :]))
        left_h[head(h), :] = hi
        left_l[head(h), :] = lo
    weigh = r.weigh
    weigh[...] = mul2((left_h[...], left_l[...]), b_ref[...], NN)
    for h in range(heads):
        weigh[head(h), :] = (weigh[head(h), :] + total[h : h + 1, :] * start_state[h]) * mine[h : h + 1, :]

    end_cotan = r.end_cotan
    back_along_x(end_cotan, r.behind, True)
    back_over_y(r.sgc)
    for j in range(pairs):
        w_along_z(j)
    in_from_x(end_cotan, r.behind)

    scaled = r.scaled
    for h in range(heads):
        scaled[head(h), :] = end_cotan[h].astype(F32) * mine[h : h + 1, :]
    e = split(scaled[...])
    over_y(grad_b[...] + mul3((xs_h[...], xs_l[...]), e, TN), r.sgb)
    hx, hz, hd = r.hx, r.hz, r.hd
    for h in range(heads):
        by_lane = jnp.sum(end_cotan[h].astype(F32) * weigh[head(h), :], axis=0, keepdims=True)
        spot = lax.broadcasted_iota(jnp.int32, (1, 128), 1) == h
        head_part[0:1, :] += jnp.where(spot, jnp.sum(by_lane, axis=1, keepdims=True), 0.0)
    hx[x] = head_part[...]
    exchange(nx, x, at_x, lambda p: hx.at[x], lambda p: hx.at[p], r.ch.hx)

    later = mul2(e, b_ref[...], NT)
    for h in range(heads):
        xf = x_ref[head(h), :].astype(F32)
        gf = cotan[head(h), :].astype(F32)
        d_later = later[head(h), :] * into[h : h + 1, :]
        d = xg[head(h), :] * into[h : h + 1, :] + d_later
        r.gx[head(h), :] = (d + r.skip[h] * gf).astype(BF16)
        to_in[h : h + 1, :] = jnp.sum(d * xf, axis=0, keepdims=True)
        to_cum[h : h + 1, :] -= jnp.sum(d_later * xf, axis=0, keepdims=True)
        closing = start_state[h] * mine[h : h + 1, :] + ends[h]
        end_part[h : h + 1, :] = jnp.sum(end_cotan[h].astype(F32) * closing, axis=0, keepdims=True)
    decay_grad = prefix_sum(to_cum[...], reverse=True) + jnp.sum(end_part[...], axis=1, keepdims=True)
    step_grad = rate * decay_grad + to_in[...] / step
    step_grad = step_grad * (grown / (1.0 + grown))
    for h in range(heads):
        r.gdt[h] = step_grad[h : h + 1, :]
    store(r.gx, r.to_gx)
    store(r.gdt, r.to_gdt)

    arrived(nx, x, at_x, lambda p: hx.at[x], lambda p: hx.at[p], r.ch.hx)
    both = hx[0]
    for j in range(1, nx):
        both = both + hx[j]
    hz[z] = both
    exchange(nz, z, at_z, lambda p: hz.at[z], lambda p: hz.at[p], r.ch.hz)
    back_over_y(r.sgb)
    in_over_y(r.sgc, r.to_gc)
    arrived(nz, z, at_z, lambda p: hz.at[z], lambda p: hz.at[p], r.ch.hz)
    both = hz[0]
    for j in range(1, nz):
        both = both + hz[j]
    hd[0] = both
    start(hd.at[0], hd.at[1], r.ch.hd, (0,), (0,), other)

    own_half = fx // 2
    gw_sum, gw_fin = r.gw_sum, r.gw_fin

    def final(d):
        return gw_sum.at[pl.ds(pl.multiple_of(d * own_half, 8), own_half), :]

    def final_copy():
        return copy(final(1 - core), gw_fin, r.ch.wf, (0,), (0,), other)

    owner = lax.rem(z + core, 2) == 0

    @pl.when(owner)
    def _():
        for k in range(1, nz):
            p = wrap(z + k, nz)
            copy(r.gw_z_out.at[0], gw_z.at[p], r.ch.wz, (0,), (p,), at_z(p)).wait_recv()
        total = gw_z[0].astype(F32)
        for j in range(1, nz):
            total = total + gw_z[j].astype(F32)
        gw_sum[...] = total
        final_copy().start()
        r.gwt[...] = gw_sum[pl.ds(pl.multiple_of(core * own_half, 8), own_half), :].astype(BF16)
        final_copy().wait_send()

    @pl.when(jnp.logical_not(owner))
    def _():
        final_copy().wait_recv()
        r.gwt[...] = gw_fin[...].astype(BF16)

    store(r.gwt, r.to_gwt)
    in_over_y(r.sgb, r.to_gb)
    copy(hd.at[0], hd.at[1], r.ch.hd, (0,), (0,), other).wait_recv()
    r.small[...] = hd[0] + hd[1]
    store(r.small, r.to_small)

    for c in stores:
        c.wait()
    for c in sends:
        c.wait_send()
    z_sent(r.ahead, False)
    z_sent(r.behind, True)
    for j in range(pairs):
        t = kept(j)

        @pl.when(t != z)
        def _(j=j, t=t):
            copy(r.gw_z_out.at[j], gw_z.at[z], r.ch.wz, (j,), (z,), at_z(t)).wait_send()


def build(nz, nx, ny, heads, width, length, state):
    rows = heads * width
    fx = rows // nx
    rp = width // nx
    pairs = ny // 2
    far = ny // 2
    piece = length // ny
    vm = pltpu.VMEM
    dma = pltpu.SemaphoreType.DMA

    def channel(sent, received=None):
        return dict(s=dma(sent), r=dma(received or sent))

    def chain(kind):
        return dict(
            got1=vm((nx, heads, rp, state), kind),
            got2=vm((nz, heads, rp, state), kind),
            got3=vm((nx, heads, rp, state), kind),
            tot=vm((heads, rp, state), kind),
            acc=vm((heads, rp, state), F32),
            ch1=channel((nx,)),
            ch2=channel((nz,)),
            ch3=channel((nx,)),
        )

    def summed():
        return dict(
            out=vm((length, state), BF16),
            got=vm((ny, piece, state), BF16),
            full=vm((length, state), BF16),
            ch=channel((ny,)),
            chf=channel((ny,)),
        )

    scratch = dict(
        g_all=vm((ny * rows, length), BF16),
        w_other=vm((rows, ny * rows // 2), BF16),
        dt_rows=vm((8, length), F32),
        rate_rows=vm((8, length), F32),
        to_in=vm((8, length), F32),
        to_cum=vm((8, length), F32),
        head_part=vm((8, 128), F32),
        dt_in=vm((heads, 1, length), F32),
        x_in=vm((rows, length), BF16),
        b_in=vm((length, state), BF16),
        c_in=vm((length, state), BF16),
        w_in=vm((rows, ny * rows // 2), BF16),
        w_block=vm((ny, rows, rows), BF16),
        cotan_f=vm((rows, length), F32),
        left_h=vm((rows, length), BF16),
        left_l=vm((rows, length), BF16),
        weigh=vm((rows, state), F32),
        grad_b=vm((length, state), F32),
        load=dma((6,)),
        end_part=vm((8, state), F32),
        decay_x=vm((nx, 8, 128), F32),
        decay_z=vm((nz, 8, 128), F32),
        hx=vm((nx, 8, 128), F32),
        hz=vm((nz, 8, 128), F32),
        hd=vm((2, 8, 128), F32),
        xs_h=vm((rows, length), BF16),
        xs_l=vm((rows, length), BF16),
        cs_h=vm((rows, length), BF16),
        cs_l=vm((rows, length), BF16),
        cotan=vm((rows, length), BF16),
        past=vm((rows, length), F32),
        xg=vm((rows, length), F32),
        near_h=vm((length, length), BF16),
        near_l=vm((length, length), BF16),
        near_gh=vm((length, length), BF16),
        near_gl=vm((length, length), BF16),
        ends=vm((heads, width, state), F32),
        start_state=vm((heads, width, state), F32),
        starts=vm((heads, width, state), BF16),
        end_cotan=vm((heads, width, state), BF16),
        s_h=vm((rows, state), BF16),
        s_l=vm((rows, state), BF16),
        scaled=vm((rows, state), F32),
        gw_out=vm((pairs, rows, rows), BF16),
        gw_dp=vm((pairs, rows, rows), BF16),
        gw_own=vm((pairs, rows, rows), F32),
        gw_send=vm((pairs, rows, rows), BF16),
        gw_x=vm((pairs, nx, fx, rows), BF16),
        gw_z=vm((nz, fx, rows), BF16),
        gw_z_out=vm((pairs, fx, rows), BF16),
        gw_sum=vm((fx, rows), F32),
        gw_fin=vm((fx // 2, rows), F32),
        ahead=chain(F32),
        behind=chain(BF16),
        sgc=summed(),
        sgb=summed(),
        ch=dict(
            g=channel((2, far, CHUNKS), (ny, CHUNKS)),
            w=channel((1,)),
            dx=channel((nx,)),
            dz=channel((nz,)),
            wd=channel((pairs,)),
            wx=channel((pairs, nx)),
            wz=channel((pairs,), (nz,)),
            wf=channel((1,)),
            hx=channel((nx,)),
            hz=channel((nz,)),
            hd=channel((1,)),
        ),
    )
    vmem = pl.BlockSpec(memory_space=pltpu.VMEM)
    smem = pl.BlockSpec(memory_space=pltpu.SMEM)
    hbm = pl.BlockSpec(memory_space=pl.ANY)
    ins = dict(x=hbm, b=hbm, c=hbm, dt=hbm, alog=smem, skip=smem, w=hbm, g=hbm)
    outs = dict(
        mixed=((rows, length), BF16),
        gx=((rows, length), BF16),
        gb=((length, state), BF16),
        gc=((length, state), BF16),
        gdt=((heads, 1, length), F32),
        gwt=((fx // 2, rows), BF16),
        small=((8, 128), F32),
    )
    scratch |= {k: vm(*v) for k, v in outs.items() if k not in ("gb", "gc")}
    scratch["stores"] = dma((len(outs),))
    placed_at = ["to_" + k for k in outs]
    held, inner = jax.tree.flatten(scratch, is_leaf=lambda v: not isinstance(v, dict))
    return pl.pallas_call(
        functools.partial(
            kernel, (nz, nx, ny, heads, width, length, state), list(ins) + placed_at, inner
        ),
        out_shape=[jax.ShapeDtypeStruct(s, d) for s, d in outs.values()],
        in_specs=list(ins.values()),
        out_specs=[hbm] * len(outs),
        scratch_shapes=held,
        compiler_params=pltpu.CompilerParams(
            collective_id=0, has_side_effects=True, vmem_limit_bytes=56 * 2**20
        ),
    )


def write_out(small, *refs):
    decay, skip, sems = refs[-3:]
    half = len(refs) // 2 - 1
    copies = [
        pltpu.make_async_copy(src, dst, sems.at[i])
        for i, (src, dst) in enumerate(zip(refs[:half], refs[half:-3], strict=True))
    ]
    for c in copies:
        c.start()
    decay[...] = small[0:1, 0 : decay.shape[1]]
    skip[...] = small[1:2, 0 : skip.shape[1]]
    for c in copies:
        c.wait()


def placed(results, small, heads):
    row = jax.ShapeDtypeStruct((1, heads), F32)
    vmem, hbm = pl.BlockSpec(memory_space=pltpu.VMEM), pl.BlockSpec(memory_space=pl.ANY)
    return pl.pallas_call(
        write_out,
        out_shape=[jax.ShapeDtypeStruct(v.shape, v.dtype) for v in results] + [row, row],
        in_specs=[vmem] * (len(results) + 1),
        out_specs=[hbm] * len(results) + [vmem, vmem],
        scratch_shapes=[pltpu.SemaphoreType.DMA((len(results),))],
    )(small, *results)


def solution(mesh):
    ny = mesh.shape["tensor"]
    nz = ny
    nx = mesh.shape["seq"] // nz

    def per_device(head_inputs, b_proj, c_proj, dt_raw, a_log, d_skip, w_out, out_grad):
        heads, length = dt_raw.shape[1:]
        width = head_inputs.shape[1] // heads
        call = build(nz, nx, ny, heads, width, length, b_proj.shape[2])
        *results, small = call(
            head_inputs[0],
            b_proj[0],
            c_proj[0],
            dt_raw.transpose(1, 0, 2),
            a_log,
            d_skip,
            w_out,
            out_grad[0],
        )
        mixed, gx, gb, gc, gdt, gwt, decay, skip = placed(results, small, heads)
        return (
            mixed[None],
            gx[None],
            gb[None],
            gc[None],
            gdt.transpose(1, 0, 2),
            decay[0],
            skip[0],
            gwt.T,
        )

    rows, tokens, per_head = P("dp", "tensor", "seq"), P("dp", "seq", None), P("tensor")
    return jax.shard_map(
        per_device,
        mesh=mesh,
        in_specs=(rows, tokens, tokens, rows, per_head, per_head, P("tensor", "dp"), rows),
        out_specs=(rows, rows, tokens, tokens, rows, per_head, per_head, P("tensor", ("seq", "dp"))),
        check_vma=False,
    )
```

```python
import functools
import types

import jax
import jax.numpy as jnp
from jax import lax
from jax.experimental import pallas as pl
from jax.experimental.pallas import tpu as pltpu
from jax.sharding import PartitionSpec as P

F32 = jnp.float32
BF16 = jnp.bfloat16
CHUNKS = 4
NN = (((1,), (0,)), ((), ()))
NT = (((1,), (1,)), ((), ()))
TN = (((0,), (0,)), ((), ()))


def mul(a, b, dims):
    return lax.dot_general(a, b, dims, preferred_element_type=F32)


def split(v):
    hi = v.astype(BF16)
    return hi, (v - hi.astype(F32)).astype(BF16)


def mul3(a, b, dims):
    return mul(a[0], b[0], dims) + mul(a[1], b[0], dims) + mul(a[0], b[1], dims)


def mul2(a, b, dims):
    return mul(a[0], b, dims) + mul(a[1], b, dims)


def prefix_sum(v, reverse=False):
    length = v.shape[1]
    lane = lax.broadcasted_iota(jnp.int32, v.shape, 1)
    shift = 1
    while shift < length:
        if reverse:
            moved = pltpu.roll(v, length - shift, 1)
            v = v + jnp.where(lane < length - shift, moved, 0.0)
        else:
            moved = pltpu.roll(v, shift, 1)
            v = v + jnp.where(lane >= shift, moved, 0.0)
        shift *= 2
    return v


def space(d):
    return types.SimpleNamespace(**{k: space(v) if isinstance(v, dict) else v for k, v in d.items()})


def kernel(dims, names, tree, *refs):
    nz, nx, ny, heads, width, length, state = dims
    r = space(
        dict(zip(names, refs[: len(names)], strict=True))
        | jax.tree.unflatten(tree, refs[len(names) :])
    )
    x_ref, b_ref, c_ref = r.x_in, r.b_in, r.c_in
    rows_all = heads * width
    rp = width // nx
    fx = rows_all // nx
    seq = lax.axis_index("seq")
    core = lax.axis_index("dp")
    y = lax.axis_index("tensor")
    z = lax.div(seq, nx)
    x = lax.rem(seq, nx)
    sends, stores = [], []

    def wrap(i, n):
        return lax.rem(i + n, n)

    def copy(src, dst, ch, out, into, where):
        return pltpu.make_async_remote_copy(
            src_ref=src,
            dst_ref=dst,
            send_sem=ch.s.at[out],
            recv_sem=ch.r.at[into],
            device_id=where,
            device_id_type=pl.DeviceIdType.MESH,
        )

    def start(*a):
        c = copy(*a)
        c.start()
        sends.append(c)

    def at_x(i):
        return {"seq": z * nx + i}

    def at_z(i):
        return {"seq": i * nx + x}

    def at_y(i):
        return {"tensor": i}

    other = {"dp": 1 - core}

    def exchange(n, me, place, src, dst, ch):
        for k in range(1, n):
            p = wrap(me + k, n)
            start(src(p), dst(me), ch, (p,), (me,), place(p))

    def arrived(n, me, place, src, dst, ch):
        for k in range(1, n):
            p = wrap(me + k, n)
            copy(src(p), dst(p), ch, (p,), (p,), place(p)).wait_recv()

    def left(n):
        for c in sends[:n]:
            c.wait_send()
        del sends[:n]

    def store(src, dst):
        c = pltpu.make_async_copy(src, dst, r.stores.at[len(stores)])
        c.start()
        stores.append(c)

    def head(h):
        return slice(h * width, (h + 1) * width)

    g_all = r.g_all
    own_rows = g_all.at[pl.ds(pl.multiple_of(y * rows_all, 16), rows_all), :]
    loads = [
        pltpu.make_async_copy(src, dst, r.load.at[i])
        for i, (src, dst) in enumerate(
            ((r.dt, r.dt_in), (r.x, x_ref), (r.b, b_ref), (r.c, c_ref), (r.w, r.w_in), (r.g, own_rows))
        )
    ]
    for c in loads:
        c.start()

    def beside(n):
        return (1,) if n == 2 else (1, n - 1) if n > 1 else ()

    barrier = pltpu.get_barrier_semaphore()
    axes = ((at_y, y, ny), (at_x, x, nx), (at_z, z, nz))
    peers = [other] + [place(wrap(i + k, n)) for place, i, n in axes for k in beside(n)]
    for p in peers:
        pl.semaphore_signal(barrier, inc=1, device_id=p, device_id_type=pl.DeviceIdType.MESH)
    pl.semaphore_wait(barrier, len(peers))

    def tell(word, stage, place, i, n):
        if stage < n // 2 - 1:
            for way, k in enumerate((1, n - 1)):
                pl.semaphore_signal(
                    word.at[stage, way],
                    inc=1,
                    device_id=place(wrap(i + k, n)),
                    device_id_type=pl.DeviceIdType.MESH,
                )

    def told(word, stage, n):
        if stage < n // 2 - 1:
            for way in range(2):
                pl.semaphore_wait(word.at[stage, way], 1)

    far = ny // 2
    tall = rows_all // CHUNKS

    def block(t, c):
        return g_all.at[pl.ds(pl.multiple_of(t * rows_all + c * tall, 16), tall), :]

    def forward(k, c, way):
        if k + 1 > far or (k + 1 == far and (c < CHUNKS // 2) != (way == 0)):
            return
        t = wrap(y - k, ny) if way == 0 else wrap(y + k, ny)
        to = wrap(y + 1, ny) if way == 0 else wrap(y - 1, ny)
        src = r.g.at[pl.ds(c * tall, tall), :] if k == 0 else block(t, c)
        start(src, block(t, c), r.ch.g, (way, k, c,), (t, c,), at_y(to))

    def block_in(t, c):
        copy(block(t, c), block(t, c), r.ch.g, (0, 0, 0,), (t, c,), at_y(y)).wait_recv()

    def relay(k, chunks):
        for c in chunks:
            if k == far:
                block_in(wrap(y + k, ny), c)
                continue
            block_in(wrap(y - k, ny), c)
            forward(k, c, 0)
            block_in(wrap(y + k, ny), c)
            forward(k, c, 1)

    for c in range(CHUNKS):
        forward(0, c, 0)
        forward(0, c, 1)
    start(r.w, r.w_other, r.ch.w, (0,), (0,), other)
    tell(r.word_x, 0, at_x, x, nx)
    tell(r.word_z, 0, at_z, z, nz)

    tile = r.dt_rows
    tile[...] = jnp.zeros_like(tile)
    loads[0].wait()
    for h in range(heads):
        tile[h : h + 1, :] = r.dt_in[h]
    rate_rows = r.rate_rows
    rate_rows[...] = jnp.zeros_like(rate_rows)
    for h in range(heads):
        rate_rows[h : h + 1, :] = -jnp.exp(jnp.full((1, length), r.alog[h], F32))
    dt = tile[...]
    rate = rate_rows[...]
    grown = jnp.exp(dt)
    step = jnp.log(1.0 + grown)
    log_decay = step * rate
    cum = prefix_sum(log_decay)
    up = jnp.exp(cum)
    into = step * jnp.exp(-cum)
    decay_x, decay_z = r.decay_x, r.decay_z
    decay_x[x] = jnp.broadcast_to(up[:, length - 1 : length], (8, 128))
    for stage in range(nx // 2 - 1):
        told(r.word_x, stage, nx)
        tell(r.word_x, stage + 1, at_x, x, nx)
    exchange(nx, x, at_x, lambda p: decay_x.at[x], lambda p: decay_x.at[p], r.ch.dx)
    told(r.word_z, 0, nz)
    tell(r.word_z, 1, at_z, z, nz)

    xs_h, xs_l = r.xs_h, r.xs_l
    loads[1].wait()
    for h in range(heads):
        hi, lo = split(x_ref[head(h), :].astype(F32) * into[h : h + 1, :])
        xs_h[head(h), :] = hi
        xs_l[head(h), :] = lo

    told(r.word_z, 1, nz)
    tell(r.word_z, 2, at_z, z, nz)

    loads[2].wait()
    part = mul2((xs_h[...], xs_l[...]), b_ref[...], NN)
    mine = decay_x[x]
    ends = r.ends
    for h in range(heads):
        ends[h] = part[head(h), :] * mine[h : h + 1, :]

    def piece(ref, i):
        return ref.at[:, pl.ds(pl.multiple_of(i * rp, rp), rp), :]

    def cut(ref, i):
        return ref[:, pl.ds(pl.multiple_of(i * rp, rp), rp), :]

    def along_x(src, st):
        got = st.got1
        exchange(nx, x, at_x, lambda p: piece(src, p), lambda p: got.at[p], st.ch1)
        got[x] = cut(src, x)

    def along_z(src, st, back):
        got, tot = st.got1, st.tot
        arrived(nx, x, at_x, lambda p: piece(src, p), lambda p: got.at[p], st.ch1)
        for h in range(heads):
            acc = jnp.zeros((rp, state), F32)
            for j in reversed(range(nx)) if back else range(nx):
                acc = acc * decay_x[j, h : h + 1, :] + got[j, h].astype(F32)
            tot[h] = acc.astype(tot.dtype)
        for k in range(1, nz):
            p = z - k if back else z + k

            @pl.when(p >= 0 if back else p < nz)
            def _(p=p):
                copy(tot, st.got2.at[z], st.ch2, (p,), (z,), at_z(p)).start()

    def back_along_x(dst, st, back):
        got, tot, acc, out = st.got1, st.tot, st.acc, st.got3
        acc[...] = jnp.zeros_like(acc)

        def gather(i, carry):
            p = nz - 1 - i if back else i
            slot = st.got2.at[p]
            copy(tot, slot, st.ch2, (p,), (p,), at_z(p)).wait_recv()
            for h in range(heads):
                acc[h] = acc[h] * decay_z[p, h : h + 1, :] + st.got2[p, h].astype(F32)
            return carry

        lax.fori_loop(0, nz - 1 - z if back else z, gather, 0)
        for h in range(heads):
            s = acc[h]
            for j in reversed(range(nx)) if back else range(nx):
                out[j, h] = s.astype(out.dtype)
                s = s * decay_x[j, h : h + 1, :] + got[j, h].astype(F32)
        for k in range(1, nx):
            p = wrap(x + k, nx)
            start(out.at[p], piece(dst, x), st.ch3, (p,), (x,), at_x(p))
        dst[:, pl.ds(pl.multiple_of(x * rp, rp), rp), :] = out[x]

    def in_from_x(dst, st):
        for k in range(1, nx):
            p = wrap(x + k, nx)
            copy(st.got3.at[p], piece(dst, p), st.ch3, (p,), (p,), at_x(p)).wait_recv()

    def z_sent(st, back):
        for k in range(1, nz):
            p = z - k if back else z + k

            @pl.when(p >= 0 if back else p < nz)
            def _(p=p):
                copy(st.tot, st.got2.at[z], st.ch2, (p,), (z,), at_z(p)).wait_send()

    along_x(ends, r.ahead)
    arrived(nx, x, at_x, lambda p: decay_x.at[x], lambda p: decay_x.at[p], r.ch.dx)
    group = decay_x[0]
    for j in range(1, nx):
        group = group * decay_x[j]
    decay_z[z] = group
    for stage in range(2, nz // 2 - 1):
        told(r.word_z, stage, nz)
        tell(r.word_z, stage + 1, at_z, z, nz)
    exchange(nz, z, at_z, lambda p: decay_z.at[z], lambda p: decay_z.at[p], r.ch.dz)

    loads[3].wait()
    earlier = lax.broadcasted_iota(jnp.int32, (length, length), 0) >= lax.broadcasted_iota(
        jnp.int32, (length, length), 1
    )
    near_h, near_l = r.near_h, r.near_l
    hi, lo = split(jnp.where(earlier, mul(c_ref[...], b_ref[...], NT), 0.0))
    near_h[...] = hi
    near_l[...] = lo

    w_block, cotan_f = r.w_block, r.cotan_f
    per_core = ny // 2

    def w_blocks(ref, d):
        for i in range(per_core):
            w_block[d * per_core + i] = ref[:, i * rows_all : (i + 1) * rows_all]

    def term(k):
        t = wrap(y + k, ny)
        return mul(w_block[t], g_all[pl.ds(pl.multiple_of(t * rows_all, 16), rows_all), :], NN)

    early, late = range(CHUNKS // 2), range(CHUNKS // 2, CHUNKS)
    if far > 1:
        relay(1, early)
    along_z(ends, r.ahead, False)
    if far > 1:
        relay(1, late)
    loads[4].wait()
    w_blocks(r.w_in, core)
    copy(r.w, r.w_other, r.ch.w, (0,), (0,), other).wait_recv()
    w_blocks(r.w_other, 1 - core)
    loads[5].wait()
    cotan_f[...] = term(0)
    if far > 1:
        cotan_f[...] += term(1) + term(-1)
    arrived(nz, z, at_z, lambda p: decay_z.at[z], lambda p: decay_z.at[p], r.ch.dz)
    start_state = r.start_state
    if far > 2:
        relay(2, range(CHUNKS))
        cotan_f[...] += term(2) + term(-2)
    back_along_x(start_state, r.ahead, False)
    if far > 3:
        relay(3, range(CHUNKS))
        cotan_f[...] += term(3) + term(-3)
    in_from_x(start_state, r.ahead)

    xt_h, xt_l = r.xt_h, r.xt_l
    xt_h[...] = xs_h[...].T
    xt_l[...] = xs_l[...].T

    s_h, s_l = split(start_state[...].reshape(rows_all, state))
    r.s_h[...] = s_h
    r.s_l[...] = s_l
    summed = mul3((xs_h[...], xs_l[...]), (near_h[...], near_l[...]), NT) + mul2((s_h, s_l), c_ref[...], NT)
    mixed = r.mixed
    past = r.past
    for h in range(heads):
        v = summed[head(h), :] * up[h : h + 1, :]
        past[head(h), :] = v
        mixed[head(h), :] = (v + r.skip[h] * x_ref[head(h), :].astype(F32)).astype(BF16)

    store(mixed, r.to_mixed)

    evens = [0] + [s * k for k in range(2, far, 2) for s in (1, -1)] + ([far] if far % 2 == 0 else [])
    odds = [s * k for k in range(1, far, 2) for s in (1, -1)] + ([far] if far % 2 == 1 else [])
    same = lax.rem(y + core, 2) == 0
    gw_dp, gw_out, gw_send, gw_x, gw_z = r.gw_dp, r.gw_out, r.gw_send, r.gw_x, r.gw_z

    def product(t):
        return mul(g_all[pl.ds(pl.multiple_of(t * rows_all, 16), rows_all), :], mixed[...], NT)

    def kept(j):
        return wrap(jnp.where(same, y + evens[j], y + odds[j]), ny)

    def w_pair(j):
        t = wrap(jnp.where(same, y + odds[j], y + evens[j]), ny)
        gw_out[j] = product(t).astype(BF16)
        start(gw_out.at[j], gw_dp.at[j], r.ch.wd, (j,), (j,), other)
        r.gw_own[j] = product(kept(j))

    def w_rows(j, p):
        return gw_send.at[j, pl.ds(pl.multiple_of(p * fx, 16), fx), :]

    def w_along_x(j):
        copy(gw_out.at[j], gw_dp.at[j], r.ch.wd, (j,), (j,), other).wait_recv()
        gw_send[j] = (r.gw_own[j] + gw_dp[j].astype(F32)).astype(BF16)
        for k in range(1, nx):
            p = wrap(x + k, nx)
            start(w_rows(j, p), gw_x.at[j, x], r.ch.wx, (j, p,), (j, x,), at_x(p))

    def w_along_z(j):
        total = gw_send[j, pl.ds(pl.multiple_of(x * fx, 16), fx), :].astype(F32)
        for k in range(1, nx):
            p = wrap(x + k, nx)
            copy(w_rows(j, p), gw_x.at[j, p], r.ch.wx, (j, p,), (j, p,), at_x(p)).wait_recv()
            total = total + gw_x[j, p].astype(F32)
        t = kept(j)
        gw_z_out = r.gw_z_out
        gw_z_out[j] = total.astype(BF16)

        @pl.when(t == z)
        def _():
            gw_z[z] = gw_z_out[j]

        @pl.when(t != z)
        def _():
            copy(gw_z_out.at[j], gw_z.at[z], r.ch.wz, (j,), (z,), at_z(t)).start()

    pairs = len(evens)
    for j in range(pairs - 1):
        w_pair(j)
    before_far = len(sends)
    relay(far, range(CHUNKS))

    cotan = r.cotan
    cotan[...] = (cotan_f[...] + term(far)).astype(BF16)
    cs_h, cs_l = r.cs_h, r.cs_l
    for h in range(heads):
        hi, lo = split(cotan[head(h), :].astype(F32) * up[h : h + 1, :])
        cs_h[head(h), :] = hi
        cs_l[head(h), :] = lo
    starts = r.starts
    starts[...] = mul2((cs_h[...], cs_l[...]), c_ref[...], NN).reshape(heads, width, state).astype(starts.dtype)
    along_x(starts, r.behind)

    for j in range(pairs - 1):
        w_along_x(j)
    w_pair(pairs - 1)

    hi, lo = split(jnp.where(earlier, mul3((cs_h[...], cs_l[...]), (xs_h[...], xs_l[...]), TN), 0.0))
    near_gh, near_gl = r.near_gh, r.near_gl
    near_gh[...] = hi
    near_gl[...] = lo
    along_z(starts, r.behind, True)

    piece_rows = length // ny

    def tokens(ref, p):
        return ref.at[pl.ds(pl.multiple_of(p * piece_rows, 16), piece_rows), :]

    grad_c = mul2((near_gh[...], near_gl[...]), b_ref[...], NN) + mul3(
        (cs_h[...], cs_l[...]), (r.s_h[...], r.s_l[...]), TN
    )

    def over_y(v, st):
        send = st.out
        send[...] = v.astype(BF16)
        exchange(ny, y, at_y, lambda p: tokens(send, p), lambda p: st.got.at[p], st.ch)

    def back_over_y(st):
        send, got, full = st.out, st.got, st.full
        arrived(ny, y, at_y, lambda p: tokens(send, p), lambda p: got.at[p], st.ch)
        total = send[pl.ds(pl.multiple_of(y * piece_rows, 16), piece_rows), :].astype(F32)
        for k in range(1, ny):
            total = total + got[wrap(y + k, ny)].astype(F32)
        full[pl.ds(pl.multiple_of(y * piece_rows, 16), piece_rows), :] = total.astype(BF16)
        exchange(ny, y, at_y, lambda p: tokens(full, y), lambda p: tokens(full, p), st.chf)

    def in_over_y(st, out):
        full = st.full
        arrived(ny, y, at_y, lambda p: tokens(full, y), lambda p: tokens(full, p), st.chf)
        store(full, out)

    over_y(grad_c, r.sgc)
    w_along_x(pairs - 1)

    xg = r.xg
    xg[...] = mul3((cs_h[...], cs_l[...]), (near_h[...], near_l[...]), NN)
    grad_b = r.grad_b
    grad_b[...] = mul2((near_gh[...], near_gl[...]), c_ref[...], TN)
    to_in, to_cum, end_part, head_part = r.to_in, r.to_cum, r.end_part, r.head_part
    for ref in (to_in, to_cum, end_part, head_part):
        ref[...] = jnp.zeros_like(ref)
    total = cum[:, length - 1 : length]
    left_h, left_l = r.left_h, r.left_l
    for h in range(heads):
        xf = x_ref[head(h), :].astype(F32)
        gf = cotan[head(h), :].astype(F32)
        xs = xf * into[h : h + 1, :]
        inner = jnp.sum(xg[head(h), :] * xs, axis=0, keepdims=True)
        here = jnp.sum(gf * r.past[head(h), :], axis=0, keepdims=True) - inner
        to_cum[h : h + 1, :] = here
        skip_sum = jnp.sum(jnp.sum(gf * xf, axis=0, keepdims=True), axis=1, keepdims=True)
        decay_sum = jnp.sum(here * cum[h : h + 1, :], axis=1, keepdims=True)
        spot = lax.broadcasted_iota(jnp.int32, (1, 128), 1) == h
        head_part[0:1, :] += jnp.where(spot, decay_sum, 0.0)
        head_part[1:2, :] += jnp.where(spot, skip_sum, 0.0)
        hi, lo = split(xs * (total[h : h + 1, :] - cum[h : h + 1, :]))
        left_h[head(h), :] = hi
        left_l[head(h), :] = lo
    weigh = r.weigh
    weigh[...] = mul2((left_h[...], left_l[...]), b_ref[...], NN)
    for h in range(heads):
        weigh[head(h), :] = (weigh[head(h), :] + total[h : h + 1, :] * start_state[h]) * mine[h : h + 1, :]

    left(before_far)
    z_sent(r.ahead, False)
    before_end = len(sends)
    end_cotan = r.end_cotan
    back_along_x(end_cotan, r.behind, True)
    back_over_y(r.sgc)
    for j in range(pairs):
        w_along_z(j)
    left(before_end)
    before_last = len(sends)
    in_from_x(end_cotan, r.behind)

    scaled = r.scaled
    for h in range(heads):
        scaled[head(h), :] = end_cotan[h].astype(F32) * mine[h : h + 1, :]
    e = split(scaled[...])
    over_y(grad_b[...] + mul3((xt_h[...], xt_l[...]), e, NN), r.sgb)
    hx, hz, hd = r.hx, r.hz, r.hd
    for h in range(heads):
        by_lane = jnp.sum(end_cotan[h].astype(F32) * weigh[head(h), :], axis=0, keepdims=True)
        spot = lax.broadcasted_iota(jnp.int32, (1, 128), 1) == h
        head_part[0:1, :] += jnp.where(spot, jnp.sum(by_lane, axis=1, keepdims=True), 0.0)
    hx[x] = head_part[...]
    exchange(nx, x, at_x, lambda p: hx.at[x], lambda p: hx.at[p], r.ch.hx)

    later = mul2(e, b_ref[...], NT)
    for h in range(heads):
        xf = x_ref[head(h), :].astype(F32)
        gf = cotan[head(h), :].astype(F32)
        d_later = later[head(h), :] * into[h : h + 1, :]
        d = xg[head(h), :] * into[h : h + 1, :] + d_later
        r.gx[head(h), :] = (d + r.skip[h] * gf).astype(BF16)
        to_in[h : h + 1, :] = jnp.sum(d * xf, axis=0, keepdims=True)
        to_cum[h : h + 1, :] -= jnp.sum(d_later * xf, axis=0, keepdims=True)
        closing = start_state[h] * mine[h : h + 1, :] + ends[h]
        end_part[h : h + 1, :] = jnp.sum(end_cotan[h].astype(F32) * closing, axis=0, keepdims=True)
    store(r.gx, r.to_gx)

    left(before_last)
    z_sent(r.behind, True)
    arrived(nx, x, at_x, lambda p: hx.at[x], lambda p: hx.at[p], r.ch.hx)
    both = hx[0]
    for j in range(1, nx):
        both = both + hx[j]
    hz[z] = both
    exchange(nz, z, at_z, lambda p: hz.at[z], lambda p: hz.at[p], r.ch.hz)
    back_over_y(r.sgb)

    decay_grad = prefix_sum(to_cum[...], reverse=True) + jnp.sum(end_part[...], axis=1, keepdims=True)
    step_grad = rate * decay_grad + to_in[...] / step
    step_grad = step_grad * (grown / (1.0 + grown))
    for h in range(heads):
        r.gdt[h] = step_grad[h : h + 1, :]
    store(r.gdt, r.to_gdt)

    own_half = fx // 2
    gw_sum, gw_fin = r.gw_sum, r.gw_fin

    def final(d):
        return gw_sum.at[pl.ds(pl.multiple_of(d * own_half, 8), own_half), :]

    def final_copy():
        return copy(final(1 - core), gw_fin, r.ch.wf, (0,), (0,), other)

    owner = lax.rem(z + core, 2) == 0

    @pl.when(owner)
    def _():
        total = jnp.zeros((fx, rows_all), F32)
        for k in range(1, nz):
            p = wrap(z + k, nz)
            copy(r.gw_z_out.at[0], gw_z.at[p], r.ch.wz, (0,), (p,), at_z(p)).wait_recv()
        for j in range(nz):
            total = total + gw_z[j].astype(F32)
        gw_sum[...] = total
        final_copy().start()
        r.gwt[...] = gw_sum[pl.ds(pl.multiple_of(core * own_half, 8), own_half), :].astype(BF16)

    in_over_y(r.sgc, r.to_gc)
    arrived(nz, z, at_z, lambda p: hz.at[z], lambda p: hz.at[p], r.ch.hz)
    both = hz[0]
    for j in range(1, nz):
        both = both + hz[j]
    hd[0] = both
    start(hd.at[0], hd.at[1], r.ch.hd, (0,), (0,), other)

    @pl.when(owner)
    def _():
        final_copy().wait_send()

    @pl.when(jnp.logical_not(owner))
    def _():
        final_copy().wait_recv()
        r.gwt[...] = gw_fin[...].astype(BF16)

    store(r.gwt, r.to_gwt)
    for j in range(pairs):
        t = kept(j)

        @pl.when(t != z)
        def _(j=j, t=t):
            copy(r.gw_z_out.at[j], gw_z.at[z], r.ch.wz, (j,), (z,), at_z(t)).wait_send()

    in_over_y(r.sgb, r.to_gb)
    copy(hd.at[0], hd.at[1], r.ch.hd, (0,), (0,), other).wait_recv()
    r.small[...] = hd[0] + hd[1]
    store(r.small, r.to_small)

    for c in stores:
        c.wait()
    left(len(sends))


def build(nz, nx, ny, heads, width, length, state):
    rows = heads * width
    fx = rows // nx
    rp = width // nx
    pairs = ny // 2
    far = ny // 2
    piece = length // ny
    vm = pltpu.VMEM
    dma = pltpu.SemaphoreType.DMA

    def channel(sent, received=None):
        return dict(s=dma(sent), r=dma(received or sent))

    def chain(kind):
        return dict(
            got1=vm((nx, heads, rp, state), kind),
            got2=vm((nz, heads, rp, state), kind),
            got3=vm((nx, heads, rp, state), kind),
            tot=vm((heads, rp, state), kind),
            acc=vm((heads, rp, state), F32),
            ch1=channel((nx,)),
            ch2=channel((nz,)),
            ch3=channel((nx,)),
        )

    def summed():
        return dict(
            out=vm((length, state), BF16),
            got=vm((ny, piece, state), BF16),
            full=vm((length, state), BF16),
            ch=channel((ny,)),
            chf=channel((ny,)),
        )

    scratch = dict(
        g_all=vm((ny * rows, length), BF16),
        w_other=vm((rows, ny * rows // 2), BF16),
        dt_rows=vm((8, length), F32),
        rate_rows=vm((8, length), F32),
        to_in=vm((8, length), F32),
        to_cum=vm((8, length), F32),
        head_part=vm((8, 128), F32),
        dt_in=vm((heads, 1, length), F32),
        x_in=vm((rows, length), BF16),
        b_in=vm((length, state), BF16),
        c_in=vm((length, state), BF16),
        w_in=vm((rows, ny * rows // 2), BF16),
        w_block=vm((ny, rows, rows), BF16),
        cotan_f=vm((rows, length), F32),
        left_h=vm((rows, length), BF16),
        left_l=vm((rows, length), BF16),
        weigh=vm((rows, state), F32),
        grad_b=vm((length, state), F32),
        load=dma((6,)),
        word_x=pltpu.SemaphoreType.REGULAR((max(nx // 2 - 1, 1), 2)),
        word_z=pltpu.SemaphoreType.REGULAR((max(nz // 2 - 1, 1), 2)),
        end_part=vm((8, state), F32),
        decay_x=vm((nx, 8, 128), F32),
        decay_z=vm((nz, 8, 128), F32),
        hx=vm((nx, 8, 128), F32),
        hz=vm((nz, 8, 128), F32),
        hd=vm((2, 8, 128), F32),
        xs_h=vm((rows, length), BF16),
        xs_l=vm((rows, length), BF16),
        cs_h=vm((rows, length), BF16),
        xt_h=vm((length, rows), BF16),
        xt_l=vm((length, rows), BF16),
        cs_l=vm((rows, length), BF16),
        cotan=vm((rows, length), BF16),
        past=vm((rows, length), F32),
        xg=vm((rows, length), F32),
        near_h=vm((length, length), BF16),
        near_l=vm((length, length), BF16),
        near_gh=vm((length, length), BF16),
        near_gl=vm((length, length), BF16),
        ends=vm((heads, width, state), F32),
        start_state=vm((heads, width, state), F32),
        starts=vm((heads, width, state), BF16),
        end_cotan=vm((heads, width, state), BF16),
        s_h=vm((rows, state), BF16),
        s_l=vm((rows, state), BF16),
        scaled=vm((rows, state), F32),
        gw_out=vm((pairs, rows, rows), BF16),
        gw_dp=vm((pairs, rows, rows), BF16),
        gw_own=vm((pairs, rows, rows), F32),
        gw_send=vm((pairs, rows, rows), BF16),
        gw_x=vm((pairs, nx, fx, rows), BF16),
        gw_z=vm((nz, fx, rows), BF16),
        gw_z_out=vm((pairs, fx, rows), BF16),
        gw_sum=vm((fx, rows), F32),
        gw_fin=vm((fx // 2, rows), F32),
        ahead=chain(F32),
        behind=chain(BF16),
        sgc=summed(),
        sgb=summed(),
        ch=dict(
            g=channel((2, far, CHUNKS), (ny, CHUNKS)),
            w=channel((1,)),
            dx=channel((nx,)),
            dz=channel((nz,)),
            wd=channel((pairs,)),
            wx=channel((pairs, nx)),
            wz=channel((pairs,), (nz,)),
            wf=channel((1,)),
            hx=channel((nx,)),
            hz=channel((nz,)),
            hd=channel((1,)),
        ),
    )
    vmem = pl.BlockSpec(memory_space=pltpu.VMEM)
    smem = pl.BlockSpec(memory_space=pltpu.SMEM)
    hbm = pl.BlockSpec(memory_space=pl.ANY)
    ins = dict(x=hbm, b=hbm, c=hbm, dt=hbm, alog=smem, skip=smem, w=hbm, g=hbm)
    outs = dict(
        mixed=((rows, length), BF16),
        gx=((rows, length), BF16),
        gb=((length, state), BF16),
        gc=((length, state), BF16),
        gdt=((heads, 1, length), F32),
        gwt=((fx // 2, rows), BF16),
        small=((8, 128), F32),
    )
    scratch |= {k: vm(*v) for k, v in outs.items() if k not in ("gb", "gc")}
    scratch["stores"] = dma((len(outs),))
    placed_at = ["to_" + k for k in outs]
    held, inner = jax.tree.flatten(scratch, is_leaf=lambda v: not isinstance(v, dict))
    return pl.pallas_call(
        functools.partial(
            kernel, (nz, nx, ny, heads, width, length, state), list(ins) + placed_at, inner
        ),
        out_shape=[jax.ShapeDtypeStruct(s, d) for s, d in outs.values()],
        in_specs=list(ins.values()),
        out_specs=[hbm] * len(outs),
        scratch_shapes=held,
        compiler_params=pltpu.CompilerParams(
            collective_id=0, has_side_effects=True, vmem_limit_bytes=56 * 2**20
        ),
    )


def write_out(small, *refs):
    decay, skip, sems = refs[-3:]
    half = len(refs) // 2 - 1
    copies = [
        pltpu.make_async_copy(src, dst, sems.at[i])
        for i, (src, dst) in enumerate(zip(refs[:half], refs[half:-3], strict=True))
    ]
    for c in copies:
        c.start()
    decay[...] = small[0:1, 0 : decay.shape[1]]
    skip[...] = small[1:2, 0 : skip.shape[1]]
    for c in copies:
        c.wait()


def placed(results, small, heads):
    row = jax.ShapeDtypeStruct((1, heads), F32)
    vmem, hbm = pl.BlockSpec(memory_space=pltpu.VMEM), pl.BlockSpec(memory_space=pl.ANY)
    return pl.pallas_call(
        write_out,
        out_shape=[jax.ShapeDtypeStruct(v.shape, v.dtype) for v in results] + [row, row],
        in_specs=[vmem] * (len(results) + 1),
        out_specs=[hbm] * len(results) + [vmem, vmem],
        scratch_shapes=[pltpu.SemaphoreType.DMA((len(results),))],
    )(small, *results)


def solution(mesh):
    ny = mesh.shape["tensor"]
    nz = ny
    nx = mesh.shape["seq"] // nz

    def per_device(head_inputs, b_proj, c_proj, dt_raw, a_log, d_skip, w_out, out_grad):
        heads, length = dt_raw.shape[1:]
        width = head_inputs.shape[1] // heads
        call = build(nz, nx, ny, heads, width, length, b_proj.shape[2])
        *results, small = call(
            head_inputs[0],
            b_proj[0],
            c_proj[0],
            dt_raw.transpose(1, 0, 2),
            a_log,
            d_skip,
            w_out,
            out_grad[0],
        )
        mixed, gx, gb, gc, gdt, gwt, decay, skip = placed(results, small, heads)
        return (
            mixed[None],
            gx[None],
            gb[None],
            gc[None],
            gdt.transpose(1, 0, 2),
            decay[0],
            skip[0],
            gwt.T,
        )

    rows, tokens, per_head = P("dp", "tensor", "seq"), P("dp", "seq", None), P("tensor")
    return jax.shard_map(
        per_device,
        mesh=mesh,
        in_specs=(rows, tokens, tokens, rows, per_head, per_head, P("tensor", "dp"), rows),
        out_specs=(rows, rows, tokens, tokens, rows, per_head, per_head, P("tensor", ("seq", "dp"))),
        check_vma=False,
    )
```

```python
import functools
import types

import jax
import jax.numpy as jnp
from jax import lax
from jax.experimental import pallas as pl
from jax.experimental.pallas import tpu as pltpu
from jax.sharding import PartitionSpec as P

F32 = jnp.float32
BF16 = jnp.bfloat16
CHUNKS = 4
NN = (((1,), (0,)), ((), ()))
NT = (((1,), (1,)), ((), ()))
TN = (((0,), (0,)), ((), ()))


def mul(a, b, dims):
    return lax.dot_general(a, b, dims, preferred_element_type=F32)


def split(v):
    hi = v.astype(BF16)
    return hi, (v - hi.astype(F32)).astype(BF16)


def mul3(a, b, dims):
    return mul(a[0], b[0], dims) + mul(a[1], b[0], dims) + mul(a[0], b[1], dims)


def mul2(a, b, dims):
    return mul(a[0], b, dims) + mul(a[1], b, dims)


def prefix_sum(v, reverse=False):
    length = v.shape[1]
    lane = lax.broadcasted_iota(jnp.int32, v.shape, 1)
    shift = 1
    while shift < length:
        if reverse:
            moved = pltpu.roll(v, length - shift, 1)
            v = v + jnp.where(lane < length - shift, moved, 0.0)
        else:
            moved = pltpu.roll(v, shift, 1)
            v = v + jnp.where(lane >= shift, moved, 0.0)
        shift *= 2
    return v


def space(d):
    return types.SimpleNamespace(**{k: space(v) if isinstance(v, dict) else v for k, v in d.items()})


def kernel(dims, names, tree, *refs):
    nz, nx, ny, heads, width, length, state = dims
    r = space(
        dict(zip(names, refs[: len(names)], strict=True))
        | jax.tree.unflatten(tree, refs[len(names) :])
    )
    x_ref, b_ref, c_ref = r.x_in, r.b_in, r.c_in
    rows_all = heads * width
    rp = width // nx
    fx = rows_all // nx
    seq = lax.axis_index("seq")
    core = lax.axis_index("dp")
    y = lax.axis_index("tensor")
    z = lax.div(seq, nx)
    x = lax.rem(seq, nx)
    sends, stores = [], []

    def wrap(i, n):
        return lax.rem(i + n, n)

    def copy(src, dst, ch, out, into, where):
        return pltpu.make_async_remote_copy(
            src_ref=src,
            dst_ref=dst,
            send_sem=ch.s.at[out],
            recv_sem=ch.r.at[into],
            device_id=where,
            device_id_type=pl.DeviceIdType.MESH,
        )

    def start(*a):
        c = copy(*a)
        c.start()
        sends.append(c)

    def at_x(i):
        return {"seq": z * nx + i}

    def at_z(i):
        return {"seq": i * nx + x}

    def at_y(i):
        return {"tensor": i}

    other = {"dp": 1 - core}

    def exchange(n, me, place, src, dst, ch):
        for k in sorted(range(1, n), key=lambda k: -min(k, n - k)):
            p = wrap(me + k, n)
            start(src(p), dst(me), ch, (p,), (me,), place(p))

    def arrived(n, me, place, src, dst, ch):
        for k in range(1, n):
            p = wrap(me + k, n)
            copy(src(p), dst(p), ch, (p,), (p,), place(p)).wait_recv()

    def left(n):
        for c in sends[:n]:
            c.wait_send()
        del sends[:n]

    def store(src, dst):
        c = pltpu.make_async_copy(src, dst, r.stores.at[len(stores)])
        c.start()
        stores.append(c)

    def head(h):
        return slice(h * width, (h + 1) * width)

    g_all = r.g_all
    own_rows = g_all.at[pl.ds(pl.multiple_of(y * rows_all, 16), rows_all), :]
    loads = [
        pltpu.make_async_copy(src, dst, r.load.at[i])
        for i, (src, dst) in enumerate(
            ((r.dt, r.dt_in), (r.x, x_ref), (r.b, b_ref), (r.c, c_ref), (r.w, r.w_in), (r.g, own_rows))
        )
    ]
    for c in loads:
        c.start()

    def beside(n):
        return (1,) if n == 2 else (1, n - 1) if n > 1 else ()

    barrier = pltpu.get_barrier_semaphore()
    axes = ((at_y, y, ny), (at_x, x, nx), (at_z, z, nz))
    peers = [other] + [place(wrap(i + k, n)) for place, i, n in axes for k in beside(n)]
    for p in peers:
        pl.semaphore_signal(barrier, inc=1, device_id=p, device_id_type=pl.DeviceIdType.MESH)
    pl.semaphore_wait(barrier, len(peers))

    def tell(word, stage, place, i, n):
        if stage < n // 2 - 1:
            for way, k in enumerate((1, n - 1)):
                pl.semaphore_signal(
                    word.at[stage, way],
                    inc=1,
                    device_id=place(wrap(i + k, n)),
                    device_id_type=pl.DeviceIdType.MESH,
                )

    def told(word, stage, n):
        if stage < n // 2 - 1:
            for way in range(2):
                pl.semaphore_wait(word.at[stage, way], 1)

    far = ny // 2
    tall = rows_all // CHUNKS

    def block(t, c):
        return g_all.at[pl.ds(pl.multiple_of(t * rows_all + c * tall, 16), tall), :]

    def forward(k, c, way):
        if k + 1 > far or (k + 1 == far and (c < CHUNKS // 2) != (way == 0)):
            return
        t = wrap(y - k, ny) if way == 0 else wrap(y + k, ny)
        to = wrap(y + 1, ny) if way == 0 else wrap(y - 1, ny)
        src = r.g.at[pl.ds(c * tall, tall), :] if k == 0 else block(t, c)
        start(src, block(t, c), r.ch.g, (way, k, c,), (t, c,), at_y(to))

    def block_in(t, c):
        copy(block(t, c), block(t, c), r.ch.g, (0, 0, 0,), (t, c,), at_y(y)).wait_recv()

    def relay(k, chunks):
        for c in chunks:
            if k == far:
                block_in(wrap(y + k, ny), c)
                continue
            block_in(wrap(y - k, ny), c)
            forward(k, c, 0)
            block_in(wrap(y + k, ny), c)
            forward(k, c, 1)

    for c in range(CHUNKS):
        forward(0, c, 0)
        forward(0, c, 1)
    start(r.w, r.w_other, r.ch.w, (0,), (0,), other)
    tell(r.word_x, 0, at_x, x, nx)
    tell(r.word_z, 0, at_z, z, nz)

    tile = r.dt_rows
    tile[...] = jnp.zeros_like(tile)
    loads[0].wait()
    for h in range(heads):
        tile[h : h + 1, :] = r.dt_in[h]
    rate_rows = r.rate_rows
    rate_rows[...] = jnp.zeros_like(rate_rows)
    for h in range(heads):
        rate_rows[h : h + 1, :] = -jnp.exp(jnp.full((1, length), r.alog[h], F32))
    dt = tile[...]
    rate = rate_rows[...]
    grown = jnp.exp(dt)
    step = jnp.log(1.0 + grown)
    log_decay = step * rate
    cum = prefix_sum(log_decay)
    up = jnp.exp(cum)
    into = step * jnp.exp(-cum)
    decay_x, decay_z = r.decay_x, r.decay_z
    decay_x[x] = jnp.broadcast_to(up[:, length - 1 : length], (8, 128))
    for stage in range(nx // 2 - 1):
        told(r.word_x, stage, nx)
        tell(r.word_x, stage + 1, at_x, x, nx)
    exchange(nx, x, at_x, lambda p: decay_x.at[x], lambda p: decay_x.at[p], r.ch.dx)
    told(r.word_z, 0, nz)
    tell(r.word_z, 1, at_z, z, nz)

    xs_h, xs_l = r.xs_h, r.xs_l
    loads[1].wait()
    for h in range(heads):
        hi, lo = split(x_ref[head(h), :].astype(F32) * into[h : h + 1, :])
        xs_h[head(h), :] = hi
        xs_l[head(h), :] = lo

    told(r.word_z, 1, nz)
    tell(r.word_z, 2, at_z, z, nz)

    loads[2].wait()
    part = mul2((xs_h[...], xs_l[...]), b_ref[...], NN)
    mine = decay_x[x]
    ends = r.ends
    for h in range(heads):
        ends[h] = part[head(h), :] * mine[h : h + 1, :]

    def piece(ref, i):
        return ref.at[:, pl.ds(pl.multiple_of(i * rp, rp), rp), :]

    def cut(ref, i):
        return ref[:, pl.ds(pl.multiple_of(i * rp, rp), rp), :]

    def along_x(src, st):
        got = st.got1
        exchange(nx, x, at_x, lambda p: piece(src, p), lambda p: got.at[p], st.ch1)
        got[x] = cut(src, x)

    def along_z(src, st, back):
        got, tot = st.got1, st.tot
        arrived(nx, x, at_x, lambda p: piece(src, p), lambda p: got.at[p], st.ch1)
        for h in range(heads):
            acc = jnp.zeros((rp, state), F32)
            for j in reversed(range(nx)) if back else range(nx):
                acc = acc * decay_x[j, h : h + 1, :] + got[j, h].astype(F32)
            tot[h] = acc.astype(tot.dtype)
        for k in sorted(range(1, nz), key=lambda k: -min(k, nz - k)):
            p = z - k if back else z + k

            @pl.when(p >= 0 if back else p < nz)
            def _(p=p):
                copy(tot, st.got2.at[z], st.ch2, (p,), (z,), at_z(p)).start()

    def back_along_x(dst, st, back):
        got, tot, acc, out = st.got1, st.tot, st.acc, st.got3
        acc[...] = jnp.zeros_like(acc)

        def gather(i, carry):
            p = nz - 1 - i if back else i
            slot = st.got2.at[p]
            copy(tot, slot, st.ch2, (p,), (p,), at_z(p)).wait_recv()
            for h in range(heads):
                acc[h] = acc[h] * decay_z[p, h : h + 1, :] + st.got2[p, h].astype(F32)
            return carry

        lax.fori_loop(0, nz - 1 - z if back else z, gather, 0)
        for h in range(heads):
            s = acc[h]
            for j in reversed(range(nx)) if back else range(nx):
                out[j, h] = s.astype(out.dtype)
                s = s * decay_x[j, h : h + 1, :] + got[j, h].astype(F32)
        for k in sorted(range(1, nx), key=lambda k: -min(k, nx - k)):
            p = wrap(x + k, nx)
            start(out.at[p], piece(dst, x), st.ch3, (p,), (x,), at_x(p))
        dst[:, pl.ds(pl.multiple_of(x * rp, rp), rp), :] = out[x]

    def in_from_x(dst, st):
        for k in range(1, nx):
            p = wrap(x + k, nx)
            copy(st.got3.at[p], piece(dst, p), st.ch3, (p,), (p,), at_x(p)).wait_recv()

    def z_sent(st, back):
        for k in range(1, nz):
            p = z - k if back else z + k

            @pl.when(p >= 0 if back else p < nz)
            def _(p=p):
                copy(st.tot, st.got2.at[z], st.ch2, (p,), (z,), at_z(p)).wait_send()

    along_x(ends, r.ahead)
    arrived(nx, x, at_x, lambda p: decay_x.at[x], lambda p: decay_x.at[p], r.ch.dx)
    group = decay_x[0]
    for j in range(1, nx):
        group = group * decay_x[j]
    decay_z[z] = group
    for stage in range(2, nz // 2 - 1):
        told(r.word_z, stage, nz)
        tell(r.word_z, stage + 1, at_z, z, nz)
    exchange(nz, z, at_z, lambda p: decay_z.at[z], lambda p: decay_z.at[p], r.ch.dz)

    loads[3].wait()
    earlier = lax.broadcasted_iota(jnp.int32, (length, length), 0) >= lax.broadcasted_iota(
        jnp.int32, (length, length), 1
    )
    near_h, near_l = r.near_h, r.near_l
    hi, lo = split(jnp.where(earlier, mul(c_ref[...], b_ref[...], NT), 0.0))
    near_h[...] = hi
    near_l[...] = lo

    w_block, cotan_f = r.w_block, r.cotan_f
    per_core = ny // 2

    def w_blocks(ref, d):
        for i in range(per_core):
            w_block[d * per_core + i] = ref[:, i * rows_all : (i + 1) * rows_all]

    def term(k):
        t = wrap(y + k, ny)
        return mul(w_block[t], g_all[pl.ds(pl.multiple_of(t * rows_all, 16), rows_all), :], NN)

    early, late = range(CHUNKS // 2), range(CHUNKS // 2, CHUNKS)
    if far > 1:
        relay(1, early)
    along_z(ends, r.ahead, False)
    if far > 1:
        relay(1, late)
    loads[4].wait()
    w_blocks(r.w_in, core)
    copy(r.w, r.w_other, r.ch.w, (0,), (0,), other).wait_recv()
    w_blocks(r.w_other, 1 - core)
    loads[5].wait()
    cotan_f[...] = term(0)
    if far > 1:
        cotan_f[...] += term(1) + term(-1)
    arrived(nz, z, at_z, lambda p: decay_z.at[z], lambda p: decay_z.at[p], r.ch.dz)
    start_state = r.start_state
    if far > 2:
        relay(2, range(CHUNKS))
        cotan_f[...] += term(2) + term(-2)
    back_along_x(start_state, r.ahead, False)
    if far > 3:
        relay(3, range(CHUNKS))
        cotan_f[...] += term(3) + term(-3)
    in_from_x(start_state, r.ahead)

    xt_h, xt_l = r.xt_h, r.xt_l
    xt_h[...] = xs_h[...].T
    xt_l[...] = xs_l[...].T

    s_h, s_l = split(start_state[...].reshape(rows_all, state))
    r.s_h[...] = s_h
    r.s_l[...] = s_l
    summed = mul3((xs_h[...], xs_l[...]), (near_h[...], near_l[...]), NT) + mul2((s_h, s_l), c_ref[...], NT)
    mixed = r.mixed
    past = r.past
    for h in range(heads):
        v = summed[head(h), :] * up[h : h + 1, :]
        past[head(h), :] = v
        mixed[head(h), :] = (v + r.skip[h] * x_ref[head(h), :].astype(F32)).astype(BF16)

    store(mixed, r.to_mixed)

    evens = [0] + [s * k for k in range(2, far, 2) for s in (1, -1)] + ([far] if far % 2 == 0 else [])
    odds = [s * k for k in range(1, far, 2) for s in (1, -1)] + ([far] if far % 2 == 1 else [])
    same = lax.rem(y + core, 2) == 0
    gw_dp, gw_out, gw_send, gw_x, gw_z = r.gw_dp, r.gw_out, r.gw_send, r.gw_x, r.gw_z

    def product(t):
        return mul(g_all[pl.ds(pl.multiple_of(t * rows_all, 16), rows_all), :], mixed[...], NT)

    def kept(j):
        return wrap(jnp.where(same, y + evens[j], y + odds[j]), ny)

    def w_pair(j):
        t = wrap(jnp.where(same, y + odds[j], y + evens[j]), ny)
        gw_out[j] = product(t).astype(BF16)
        start(gw_out.at[j], gw_dp.at[j], r.ch.wd, (j,), (j,), other)
        r.gw_own[j] = product(kept(j))

    def w_rows(j, p):
        return gw_send.at[j, pl.ds(pl.multiple_of(p * fx, 16), fx), :]

    def w_along_x(j):
        copy(gw_out.at[j], gw_dp.at[j], r.ch.wd, (j,), (j,), other).wait_recv()
        gw_send[j] = (r.gw_own[j] + gw_dp[j].astype(F32)).astype(BF16)
        for k in range(1, nx):
            p = wrap(x + k, nx)
            start(w_rows(j, p), gw_x.at[j, x], r.ch.wx, (j, p,), (j, x,), at_x(p))

    def w_along_z(j):
        total = gw_send[j, pl.ds(pl.multiple_of(x * fx, 16), fx), :].astype(F32)
        for k in range(1, nx):
            p = wrap(x + k, nx)
            copy(w_rows(j, p), gw_x.at[j, p], r.ch.wx, (j, p,), (j, p,), at_x(p)).wait_recv()
            total = total + gw_x[j, p].astype(F32)
        t = kept(j)
        gw_z_out = r.gw_z_out
        gw_z_out[j] = total.astype(BF16)

        @pl.when(t == z)
        def _():
            gw_z[z] = gw_z_out[j]

        @pl.when(t != z)
        def _():
            copy(gw_z_out.at[j], gw_z.at[z], r.ch.wz, (j,), (z,), at_z(t)).start()

    pairs = len(evens)
    for j in range(pairs - 1):
        w_pair(j)
    before_far = len(sends)
    relay(far, range(CHUNKS))

    cotan = r.cotan
    cotan[...] = (cotan_f[...] + term(far)).astype(BF16)
    cs_h, cs_l = r.cs_h, r.cs_l
    for h in range(heads):
        hi, lo = split(cotan[head(h), :].astype(F32) * up[h : h + 1, :])
        cs_h[head(h), :] = hi
        cs_l[head(h), :] = lo
    starts = r.starts
    starts[...] = mul2((cs_h[...], cs_l[...]), c_ref[...], NN).reshape(heads, width, state).astype(starts.dtype)
    along_x(starts, r.behind)

    w_pair(pairs - 1)

    hi, lo = split(jnp.where(earlier, mul3((cs_h[...], cs_l[...]), (xs_h[...], xs_l[...]), TN), 0.0))
    near_gh, near_gl = r.near_gh, r.near_gl
    near_gh[...] = hi
    near_gl[...] = lo
    along_z(starts, r.behind, True)
    soon = min(3, pairs)
    for j in range(soon):
        w_along_x(j)

    piece_rows = length // ny

    def tokens(ref, p):
        return ref.at[pl.ds(pl.multiple_of(p * piece_rows, 16), piece_rows), :]

    grad_c = mul2((near_gh[...], near_gl[...]), b_ref[...], NN) + mul3(
        (cs_h[...], cs_l[...]), (r.s_h[...], r.s_l[...]), TN
    )

    def over_y(v, st):
        send = st.out
        send[...] = v.astype(BF16)
        exchange(ny, y, at_y, lambda p: tokens(send, p), lambda p: st.got.at[p], st.ch)

    def back_over_y(st):
        send, got, full = st.out, st.got, st.full
        arrived(ny, y, at_y, lambda p: tokens(send, p), lambda p: got.at[p], st.ch)
        total = send[pl.ds(pl.multiple_of(y * piece_rows, 16), piece_rows), :].astype(F32)
        for k in range(1, ny):
            total = total + got[wrap(y + k, ny)].astype(F32)
        full[pl.ds(pl.multiple_of(y * piece_rows, 16), piece_rows), :] = total.astype(BF16)
        exchange(ny, y, at_y, lambda p: tokens(full, y), lambda p: tokens(full, p), st.chf)

    def in_over_y(st, out):
        full = st.full
        arrived(ny, y, at_y, lambda p: tokens(full, y), lambda p: tokens(full, p), st.chf)
        store(full, out)

    over_y(grad_c, r.sgc)

    xg = r.xg
    xg[...] = mul3((cs_h[...], cs_l[...]), (near_h[...], near_l[...]), NN)
    grad_b = r.grad_b
    grad_b[...] = mul2((near_gh[...], near_gl[...]), c_ref[...], TN)
    to_in, to_cum, end_part, head_part = r.to_in, r.to_cum, r.end_part, r.head_part
    for ref in (to_in, to_cum, end_part, head_part):
        ref[...] = jnp.zeros_like(ref)
    total = cum[:, length - 1 : length]
    left_h, left_l = r.left_h, r.left_l
    for h in range(heads):
        xf = x_ref[head(h), :].astype(F32)
        gf = cotan[head(h), :].astype(F32)
        xs = xf * into[h : h + 1, :]
        inner = jnp.sum(xg[head(h), :] * xs, axis=0, keepdims=True)
        here = jnp.sum(gf * r.past[head(h), :], axis=0, keepdims=True) - inner
        to_cum[h : h + 1, :] = here
        skip_sum = jnp.sum(jnp.sum(gf * xf, axis=0, keepdims=True), axis=1, keepdims=True)
        decay_sum = jnp.sum(here * cum[h : h + 1, :], axis=1, keepdims=True)
        spot = lax.broadcasted_iota(jnp.int32, (1, 128), 1) == h
        head_part[0:1, :] += jnp.where(spot, decay_sum, 0.0)
        head_part[1:2, :] += jnp.where(spot, skip_sum, 0.0)
        hi, lo = split(xs * (total[h : h + 1, :] - cum[h : h + 1, :]))
        left_h[head(h), :] = hi
        left_l[head(h), :] = lo
    weigh = r.weigh
    weigh[...] = mul2((left_h[...], left_l[...]), b_ref[...], NN)
    for h in range(heads):
        weigh[head(h), :] = (weigh[head(h), :] + total[h : h + 1, :] * start_state[h]) * mine[h : h + 1, :]

    left(before_far)
    z_sent(r.ahead, False)
    before_end = len(sends)
    end_cotan = r.end_cotan
    back_along_x(end_cotan, r.behind, True)
    for j in range(soon, pairs):
        w_along_x(j)
    back_over_y(r.sgc)
    for j in range(soon):
        w_along_z(j)
    left(before_end)
    before_last = len(sends)
    in_from_x(end_cotan, r.behind)

    scaled = r.scaled
    for h in range(heads):
        scaled[head(h), :] = end_cotan[h].astype(F32) * mine[h : h + 1, :]
    e = split(scaled[...])
    over_y(grad_b[...] + mul3((xt_h[...], xt_l[...]), e, NN), r.sgb)
    hx, hz, hd = r.hx, r.hz, r.hd
    for h in range(heads):
        by_lane = jnp.sum(end_cotan[h].astype(F32) * weigh[head(h), :], axis=0, keepdims=True)
        spot = lax.broadcasted_iota(jnp.int32, (1, 128), 1) == h
        head_part[0:1, :] += jnp.where(spot, jnp.sum(by_lane, axis=1, keepdims=True), 0.0)
    hx[x] = head_part[...]
    exchange(nx, x, at_x, lambda p: hx.at[x], lambda p: hx.at[p], r.ch.hx)

    later = mul2(e, b_ref[...], NT)
    for h in range(heads):
        xf = x_ref[head(h), :].astype(F32)
        gf = cotan[head(h), :].astype(F32)
        d_later = later[head(h), :] * into[h : h + 1, :]
        d = xg[head(h), :] * into[h : h + 1, :] + d_later
        r.gx[head(h), :] = (d + r.skip[h] * gf).astype(BF16)
        to_in[h : h + 1, :] = jnp.sum(d * xf, axis=0, keepdims=True)
        to_cum[h : h + 1, :] -= jnp.sum(d_later * xf, axis=0, keepdims=True)
        closing = start_state[h] * mine[h : h + 1, :] + ends[h]
        end_part[h : h + 1, :] = jnp.sum(end_cotan[h].astype(F32) * closing, axis=0, keepdims=True)
    store(r.gx, r.to_gx)
    for j in range(soon, pairs):
        w_along_z(j)

    left(before_last)
    z_sent(r.behind, True)
    arrived(nx, x, at_x, lambda p: hx.at[x], lambda p: hx.at[p], r.ch.hx)
    both = hx[0]
    for j in range(1, nx):
        both = both + hx[j]
    hz[z] = both
    exchange(nz, z, at_z, lambda p: hz.at[z], lambda p: hz.at[p], r.ch.hz)
    back_over_y(r.sgb)

    decay_grad = prefix_sum(to_cum[...], reverse=True) + jnp.sum(end_part[...], axis=1, keepdims=True)
    step_grad = rate * decay_grad + to_in[...] / step
    step_grad = step_grad * (grown / (1.0 + grown))
    for h in range(heads):
        r.gdt[h] = step_grad[h : h + 1, :]
    store(r.gdt, r.to_gdt)

    own_half = fx // 2
    gw_sum, gw_fin = r.gw_sum, r.gw_fin

    def final(d):
        return gw_sum.at[pl.ds(pl.multiple_of(d * own_half, 8), own_half), :]

    def final_copy():
        return copy(final(1 - core), gw_fin, r.ch.wf, (0,), (0,), other)

    owner = lax.rem(z + core, 2) == 0

    @pl.when(owner)
    def _():
        total = jnp.zeros((fx, rows_all), F32)
        for k in range(1, nz):
            p = wrap(z + k, nz)
            copy(r.gw_z_out.at[0], gw_z.at[p], r.ch.wz, (0,), (p,), at_z(p)).wait_recv()
        for j in range(nz):
            total = total + gw_z[j].astype(F32)
        gw_sum[...] = total
        final_copy().start()
        r.gwt[...] = gw_sum[pl.ds(pl.multiple_of(core * own_half, 8), own_half), :].astype(BF16)

    in_over_y(r.sgc, r.to_gc)
    arrived(nz, z, at_z, lambda p: hz.at[z], lambda p: hz.at[p], r.ch.hz)
    both = hz[0]
    for j in range(1, nz):
        both = both + hz[j]
    hd[0] = both
    start(hd.at[0], hd.at[1], r.ch.hd, (0,), (0,), other)

    @pl.when(owner)
    def _():
        final_copy().wait_send()

    @pl.when(jnp.logical_not(owner))
    def _():
        final_copy().wait_recv()
        r.gwt[...] = gw_fin[...].astype(BF16)

    store(r.gwt, r.to_gwt)
    for j in range(pairs):
        t = kept(j)

        @pl.when(t != z)
        def _(j=j, t=t):
            copy(r.gw_z_out.at[j], gw_z.at[z], r.ch.wz, (j,), (z,), at_z(t)).wait_send()

    in_over_y(r.sgb, r.to_gb)
    copy(hd.at[0], hd.at[1], r.ch.hd, (0,), (0,), other).wait_recv()
    r.small[...] = hd[0] + hd[1]
    store(r.small, r.to_small)

    for c in stores:
        c.wait()
    left(len(sends))


def build(nz, nx, ny, heads, width, length, state):
    rows = heads * width
    fx = rows // nx
    rp = width // nx
    pairs = ny // 2
    far = ny // 2
    piece = length // ny
    vm = pltpu.VMEM
    dma = pltpu.SemaphoreType.DMA

    def channel(sent, received=None):
        return dict(s=dma(sent), r=dma(received or sent))

    def chain(kind):
        return dict(
            got1=vm((nx, heads, rp, state), kind),
            got2=vm((nz, heads, rp, state), kind),
            got3=vm((nx, heads, rp, state), kind),
            tot=vm((heads, rp, state), kind),
            acc=vm((heads, rp, state), F32),
            ch1=channel((nx,)),
            ch2=channel((nz,)),
            ch3=channel((nx,)),
        )

    def summed():
        return dict(
            out=vm((length, state), BF16),
            got=vm((ny, piece, state), BF16),
            full=vm((length, state), BF16),
            ch=channel((ny,)),
            chf=channel((ny,)),
        )

    scratch = dict(
        g_all=vm((ny * rows, length), BF16),
        w_other=vm((rows, ny * rows // 2), BF16),
        dt_rows=vm((8, length), F32),
        rate_rows=vm((8, length), F32),
        to_in=vm((8, length), F32),
        to_cum=vm((8, length), F32),
        head_part=vm((8, 128), F32),
        dt_in=vm((heads, 1, length), F32),
        x_in=vm((rows, length), BF16),
        b_in=vm((length, state), BF16),
        c_in=vm((length, state), BF16),
        w_in=vm((rows, ny * rows // 2), BF16),
        w_block=vm((ny, rows, rows), BF16),
        cotan_f=vm((rows, length), F32),
        left_h=vm((rows, length), BF16),
        left_l=vm((rows, length), BF16),
        weigh=vm((rows, state), F32),
        grad_b=vm((length, state), F32),
        load=dma((6,)),
        word_x=pltpu.SemaphoreType.REGULAR((max(nx // 2 - 1, 1), 2)),
        word_z=pltpu.SemaphoreType.REGULAR((max(nz // 2 - 1, 1), 2)),
        end_part=vm((8, state), F32),
        decay_x=vm((nx, 8, 128), F32),
        decay_z=vm((nz, 8, 128), F32),
        hx=vm((nx, 8, 128), F32),
        hz=vm((nz, 8, 128), F32),
        hd=vm((2, 8, 128), F32),
        xs_h=vm((rows, length), BF16),
        xs_l=vm((rows, length), BF16),
        cs_h=vm((rows, length), BF16),
        xt_h=vm((length, rows), BF16),
        xt_l=vm((length, rows), BF16),
        cs_l=vm((rows, length), BF16),
        cotan=vm((rows, length), BF16),
        past=vm((rows, length), F32),
        xg=vm((rows, length), F32),
        near_h=vm((length, length), BF16),
        near_l=vm((length, length), BF16),
        near_gh=vm((length, length), BF16),
        near_gl=vm((length, length), BF16),
        ends=vm((heads, width, state), F32),
        start_state=vm((heads, width, state), F32),
        starts=vm((heads, width, state), BF16),
        end_cotan=vm((heads, width, state), BF16),
        s_h=vm((rows, state), BF16),
        s_l=vm((rows, state), BF16),
        scaled=vm((rows, state), F32),
        gw_out=vm((pairs, rows, rows), BF16),
        gw_dp=vm((pairs, rows, rows), BF16),
        gw_own=vm((pairs, rows, rows), F32),
        gw_send=vm((pairs, rows, rows), BF16),
        gw_x=vm((pairs, nx, fx, rows), BF16),
        gw_z=vm((nz, fx, rows), BF16),
        gw_z_out=vm((pairs, fx, rows), BF16),
        gw_sum=vm((fx, rows), F32),
        gw_fin=vm((fx // 2, rows), F32),
        ahead=chain(F32),
        behind=chain(BF16),
        sgc=summed(),
        sgb=summed(),
        ch=dict(
            g=channel((2, far, CHUNKS), (ny, CHUNKS)),
            w=channel((1,)),
            dx=channel((nx,)),
            dz=channel((nz,)),
            wd=channel((pairs,)),
            wx=channel((pairs, nx)),
            wz=channel((pairs,), (nz,)),
            wf=channel((1,)),
            hx=channel((nx,)),
            hz=channel((nz,)),
            hd=channel((1,)),
        ),
    )
    vmem = pl.BlockSpec(memory_space=pltpu.VMEM)
    smem = pl.BlockSpec(memory_space=pltpu.SMEM)
    hbm = pl.BlockSpec(memory_space=pl.ANY)
    ins = dict(x=hbm, b=hbm, c=hbm, dt=hbm, alog=smem, skip=smem, w=hbm, g=hbm)
    outs = dict(
        mixed=((rows, length), BF16),
        gx=((rows, length), BF16),
        gb=((length, state), BF16),
        gc=((length, state), BF16),
        gdt=((heads, 1, length), F32),
        gwt=((fx // 2, rows), BF16),
        small=((8, 128), F32),
    )
    scratch |= {k: vm(*v) for k, v in outs.items() if k not in ("gb", "gc")}
    scratch["stores"] = dma((len(outs),))
    placed_at = ["to_" + k for k in outs]
    held, inner = jax.tree.flatten(scratch, is_leaf=lambda v: not isinstance(v, dict))
    return pl.pallas_call(
        functools.partial(
            kernel, (nz, nx, ny, heads, width, length, state), list(ins) + placed_at, inner
        ),
        out_shape=[jax.ShapeDtypeStruct(s, d) for s, d in outs.values()],
        in_specs=list(ins.values()),
        out_specs=[hbm] * len(outs),
        scratch_shapes=held,
        compiler_params=pltpu.CompilerParams(
            collective_id=0, has_side_effects=True, vmem_limit_bytes=56 * 2**20
        ),
    )


def write_out(small, *refs):
    decay, skip, sems = refs[-3:]
    half = len(refs) // 2 - 1
    copies = [
        pltpu.make_async_copy(src, dst, sems.at[i])
        for i, (src, dst) in enumerate(zip(refs[:half], refs[half:-3], strict=True))
    ]
    for c in copies:
        c.start()
    decay[...] = small[0:1, 0 : decay.shape[1]]
    skip[...] = small[1:2, 0 : skip.shape[1]]
    for c in copies:
        c.wait()


def placed(results, small, heads):
    row = jax.ShapeDtypeStruct((1, heads), F32)
    vmem, hbm = pl.BlockSpec(memory_space=pltpu.VMEM), pl.BlockSpec(memory_space=pl.ANY)
    return pl.pallas_call(
        write_out,
        out_shape=[jax.ShapeDtypeStruct(v.shape, v.dtype) for v in results] + [row, row],
        in_specs=[vmem] * (len(results) + 1),
        out_specs=[hbm] * len(results) + [vmem, vmem],
        scratch_shapes=[pltpu.SemaphoreType.DMA((len(results),))],
    )(small, *results)


def solution(mesh):
    ny = mesh.shape["tensor"]
    nz = ny
    nx = mesh.shape["seq"] // nz

    def per_device(head_inputs, b_proj, c_proj, dt_raw, a_log, d_skip, w_out, out_grad):
        heads, length = dt_raw.shape[1:]
        width = head_inputs.shape[1] // heads
        call = build(nz, nx, ny, heads, width, length, b_proj.shape[2])
        *results, small = call(
            head_inputs[0],
            b_proj[0],
            c_proj[0],
            dt_raw.transpose(1, 0, 2),
            a_log,
            d_skip,
            w_out,
            out_grad[0],
        )
        mixed, gx, gb, gc, gdt, gwt, decay, skip = placed(results, small, heads)
        return (
            mixed[None],
            gx[None],
            gb[None],
            gc[None],
            gdt.transpose(1, 0, 2),
            decay[0],
            skip[0],
            gwt.T,
        )

    rows, tokens, per_head = P("dp", "tensor", "seq"), P("dp", "seq", None), P("tensor")
    return jax.shard_map(
        per_device,
        mesh=mesh,
        in_specs=(rows, tokens, tokens, rows, per_head, per_head, P("tensor", "dp"), rows),
        out_specs=(rows, rows, tokens, tokens, rows, per_head, per_head, P("tensor", ("seq", "dp"))),
        check_vma=False,
    )
```
